512 devices in a mesh: row: 16 (over x, y_hi, core), col: 32 (over y_lo, z).
Axes of the slice: x: 4, y: 8 (y_hi: 2, y_lo: 4; y = y_hi * 4 + y_lo), z: 8, core: 2. Of those that a mesh axis runs over, the one named last changes fastest.
Arguments:
- train_features: float32 [4096, 8192], P('col', 'row'), may hold values from -6 to 6
- inverse: float32 [8192, 8192], P('row', 'col'), may hold values from -0.0625 to 0.0625
- test_features: float32 [1024, 8192], P('row', 'col'), may hold values from -0.0625 to 0.0625
Outputs:
- scores: float32 [1024, 4096], P('col', 'row')
The draws below stay inside these ranges and needn't reach their ends.
All inputs are finite; a program needn't handle non-finite values.
Results may differ from the reference program's by a relative error of at most 0.000071.
Values sent between devices are 32-bit elements; how exact they have to be, the bound alone decides.
A program may use at most 64 MiB of HBM per device.

```python
import jax
import jax.numpy as jnp
from jax import lax

P_SIZE = 8192
NTRAIN = 4096
NTEST = 1024


def shard_levels(rng, dims, pieces, least, largest):
    factor_of = 1.0
    for axis_at, blocks in pieces:
        heights = jax.random.uniform(jax.random.fold_in(jax.random.fold_in(rng, 6), axis_at), (blocks,), jnp.float32, least / len(pieces), largest / len(pieces))
        factor_of = factor_of * jnp.repeat(jnp.exp(heights), dims[axis_at] // blocks).reshape((-1,) + (1,) * (len(dims) - 1 - axis_at))
    return factor_of


def gaussian(own_key, dims, spread, bound, pieces=(), kind=jnp.bfloat16):
    gain = shard_levels(own_key, dims, pieces, -0.22, 0.18) if pieces else 1.0
    array = jax.random.normal(own_key, dims, jnp.float32) * spread * gain
    return jnp.minimum(jnp.maximum(array, -bound), bound).astype(kind)


def setup_inputs(seed: int = 0) -> dict:
    arg_keys = jax.random.split(jax.random.key(seed), 4)
    train_features = gaussian(arg_keys[0], (NTRAIN, P_SIZE), 1.0, 6.0, ((0, 32), (1, 16)), jnp.float32)
    inverse = gaussian(arg_keys[1], (P_SIZE, P_SIZE), P_SIZE ** -0.5, 0.0625, ((0, 16), (1, 32)), jnp.float32)
    test_features = gaussian(arg_keys[2], (NTEST, P_SIZE), P_SIZE ** -0.5, 0.0625, ((0, 16), (1, 32)), jnp.float32)
    return dict(train_features=train_features, inverse=inverse, test_features=test_features)


def reference(train_features, inverse, test_features):
    whitened = jnp.dot(train_features, inverse, precision=lax.Precision.HIGHEST, preferred_element_type=jnp.float32)
    return lax.dot_general(test_features, whitened, (((1,), (1,)), ((), ())), precision=lax.Precision.HIGHEST, preferred_element_type=jnp.float32)
```

```python
import functools

import jax
import jax.numpy as jnp
from jax import lax
from jax.experimental import pallas as pl
from jax.experimental.pallas import tpu as pltpu
from jax.sharding import PartitionSpec as P

MESH = pl.DeviceIdType.MESH
F32 = jnp.float32
BF16 = jnp.bfloat16


def split(value):
    high = value.astype(BF16)
    return high, (value - high.astype(F32)).astype(BF16)


def dot_nt(left, right):
    def product(a, b):
        return lax.dot_general(a, b, (((1,), (1,)), ((), ())), preferred_element_type=F32)

    return product(left[0], right[1]) + product(left[1], right[0]) + product(left[0], right[0])


def device(x, yh, core, yl, z):
    return ((x * 2 + yh) * 2 + core, yl * 8 + z)


def kernel(
    x_ref, m_ref, t_ref, o_ref,
    mb, xb, ty, tb, u, rs, ag, op, fr,
    local_sem, m_send, m_recv, x_send, x_recv, ty_send, ty_recv, t_send, t_recv,
    rs_send, rs_recv, ag_send, ag_recv, f_send, f_recv,
):
    r = lax.axis_index("row")
    c = lax.axis_index("col")
    k = r % 2
    yh = (r // 2) % 2
    x = r // 4
    rp = r // 2
    yl = c // 8
    z = c % 8
    p = z % 2
    w = z // 2

    def remote(src, dst, send, recv, to):
        return pltpu.make_async_remote_copy(
            src_ref=src, dst_ref=dst, send_sem=send, recv_sem=recv, device_id=to, device_id_type=MESH
        )

    sibling = device(x, yh, 1 - k, yl, z)
    across = device(x, 1 - yh, k, yl, z)
    partner = device(x, yh, k, yl, z + 1 - 2 * p)

    def along_x(dx, dp):
        zz = z if dp == 0 else z + 1 - 2 * p
        return device((x + dx) % 4, yh, k, yl, zz)

    def along_col(dy, dw):
        return device(x, yh, k, (yl + dy) % 4, 2 * ((w + dw) % 4) + p)

    barrier = pltpu.get_barrier_semaphore()
    greeted = [across, sibling]
    greeted += [along_x(dx, dp) for dx in range(4) for dp in range(2) if dx or dp]
    greeted += [along_col(dy, dw) for dy in range(4) for dw in range(4) if dy or dw]
    for to in greeted:
        pl.semaphore_signal(barrier, inc=1, device_id=to, device_id_type=MESH)

    own_m = pltpu.make_async_copy(m_ref, mb.at[0, 0], local_sem.at[0])
    own_x = pltpu.make_async_copy(x_ref, xb.at[0, 0], local_sem.at[1])
    own_t = pltpu.make_async_copy(
        t_ref.at[pl.ds(pl.multiple_of(32 * p, 32), 32)],
        tb.at[0, pl.ds(pl.multiple_of(32 * rp, 32), 32)],
        local_sem.at[2],
    )
    own_m.start()
    own_x.start()
    own_t.start()

    pl.semaphore_wait(barrier, len(greeted))

    copy_ty = remote(t_ref, ty, ty_send, ty_recv, across)
    copy_ty.start()
    t_copies = []

    def send_t(block_ref, b):
        rows = pl.ds(pl.multiple_of(32 * (2 * x + (yh if b == 0 else 1 - yh)), 32), 32)
        for dx in (2, 1, 3, 0):
            for dp in range(2):
                if dx == 0 and dp == 0:
                    continue
                half = p if dp == 0 else 1 - p
                n = (b * 4 + dx) * 2 + dp
                copy = remote(
                    block_ref.at[pl.ds(pl.multiple_of(32 * half, 32), 32)],
                    tb.at[dp, rows], t_send.at[n], t_recv.at[n], along_x(dx, dp),
                )
                copy.start()
                t_copies.append(copy)

    send_t(t_ref, 0)
    copy_mp = remote(m_ref, mb.at[1, 0], m_send.at[0], m_recv.at[0], partner)
    copy_mp.start()
    copy_ms = remote(m_ref, mb.at[0, 1], m_send.at[1], m_recv.at[1], sibling)
    copy_ms.start()
    copy_ty.wait_recv()
    send_t(ty, 1)
    own_ty = pltpu.make_async_copy(
        ty.at[pl.ds(pl.multiple_of(32 * p, 32), 32)],
        tb.at[0, pl.ds(pl.multiple_of(32 * (2 * x + 1 - yh), 32), 32)],
        local_sem.at[3],
    )
    own_ty.start()

    x_copies = []
    for d in (1, 2, 3):
        to = device(x, yh, k, (yl + d) % 4, z)
        copy = remote(x_ref, xb.at[4 - d, 0], x_send.at[4 - d], x_recv.at[4 - d], to)
        copy.start()
        x_copies.append(copy)
    copy_xs = remote(x_ref, xb.at[0, 1], x_send.at[4], x_recv.at[4], sibling)
    copy_xs.start()

    own_m.wait()
    own_t.wait()
    own_ty.wait()
    for copy in t_copies:
        copy.wait_recv()
    copy_mp.wait_recv()
    copy_mr = remote(mb.at[1, 0], mb.at[1, 1], m_send.at[2], m_recv.at[2], sibling)
    copy_mr.start()

    t_halves = [split(tb[q]) for q in range(2)]
    rs_copies = [[], []]
    for cr in range(2):
        if cr == 1:
            copy_ms.wait_recv()
            copy_mr.wait_recv()
        u[cr] = dot_nt(t_halves[0], split(mb[0, cr])) + dot_nt(t_halves[1], split(mb[1, cr]))
        for dw in (2, 1, 3, 0):
            for dy in (2, 1, 3, 0):
                e = dy * 4 + dw
                if e == 0:
                    continue
                m = 4 * ((yl + dy) % 4) + (w + dw) % 4
                copy = remote(
                    u.at[cr, pl.ds(pl.multiple_of(16 * m, 16), 16)], rs.at[cr, e],
                    rs_send.at[cr, e], rs_recv.at[cr, e], along_col(dy, dw),
                )
                copy.start()
                rs_copies[cr].append(copy)

    mine = pl.ds(pl.multiple_of(16 * (4 * yl + w), 16), 16)
    slot = (z // 4) * 4 + (z % 2) * 2 + (z // 2) % 2
    slot_rows = pl.ds(pl.multiple_of(16 * slot, 16), 16)
    ag_copies = [[], []]
    for cr in range(2):
        for copy in rs_copies[cr]:
            copy.wait_recv()
        total = u[cr, mine]
        for e in range(1, 16):
            total = total + rs[cr, e]
        ag[cr, slot_rows] = total
        for dz in (4, 3, 5, 2, 6, 1, 7):
            to = device(x, yh, k, yl, (z + dz) % 8)
            copy = remote(
                ag.at[cr, slot_rows], ag.at[cr, slot_rows], ag_send.at[cr, dz], ag_recv.at[cr, dz], to
            )
            copy.start()
            ag_copies[cr].append(copy)
        if cr == 0:
            own_x.wait()
            relays = []
            for copy, d in zip(x_copies, (3, 2, 1)):
                copy.wait_recv()
                relay = remote(xb.at[d, 0], xb.at[d, 1], x_send.at[4 + d], x_recv.at[4 + d], sibling)
                relay.start()
                relays.append(relay)
            copy_xs.wait_recv()
            for relay in relays:
                relay.wait_recv()

    for cr in range(2):
        for copy in ag_copies[cr]:
            copy.wait_recv()
    a = [split(ag[cr]) for cr in range(2)]

    def same(to):
        return jnp.logical_and(to[0] == r, to[1] == c)

    finals = []
    for d in range(4):
        op[d] = dot_nt(a[0], split(xb[d, 0])) + dot_nt(a[1], split(xb[d, 1]))
        for g in range(2):
            for q in range(2):
                n = (d * 2 + g) * 2 + q
                to = device((yl + d) % 4, z // 4, (z // 2) % 2, yl, 4 * g + 2 * k + q)
                rows = pl.ds(32 * (2 * g + q), 32)
                here = same(to)
                copy = remote(
                    op.at[d, rows], fr.at[rp, z % 2], f_send.at[n], f_recv.at[rp, z % 2], to
                )
                finals.append((here, copy))

                @pl.when(jnp.logical_not(here))
                def _(copy=copy):
                    copy.start()

                @pl.when(here)
                def _(d=d, rows=rows):
                    fr[rp, z % 2] = op[d, rows]

    for half in range(2):
        total = None
        for s in range(8):
            z_from = 4 * yh + 2 * k + half
            here = jnp.logical_and(
                jnp.logical_and(rp == s, z_from == z), k == (z // 2) % 2
            )
            arrival = remote(
                op.at[0, pl.ds(0, 32)], fr.at[s, half], f_send.at[0], f_recv.at[s, half], sibling
            )

            @pl.when(jnp.logical_not(here))
            def _(arrival=arrival):
                arrival.wait_recv()

        total = fr[0, half]
        for s in range(1, 8):
            total = total + fr[s, half]
        o_ref[:, pl.ds(128 * half, 128)] = total

    copy_ty.wait_send()
    for copy in t_copies + x_copies + relays + rs_copies[0] + rs_copies[1] + ag_copies[0] + ag_copies[1]:
        copy.wait_send()
    for copy in (copy_mp, copy_ms, copy_mr, copy_xs):
        copy.wait_send()
    for here, copy in finals:

        @pl.when(jnp.logical_not(here))
        def _(copy=copy):
            copy.wait_send()


def on_device(train_features, inverse, test_features):
    vmem = pltpu.VMEM
    dma = pltpu.SemaphoreType.DMA
    return pl.pallas_call(
        kernel,
        out_shape=jax.ShapeDtypeStruct((32, 256), F32),
        in_specs=[pl.BlockSpec(memory_space=pl.ANY)] * 3,
        out_specs=pl.BlockSpec(memory_space=pltpu.VMEM),
        scratch_shapes=[
            vmem((2, 2, 512, 256), F32),
            vmem((4, 2, 128, 512), F32),
            vmem((64, 256), F32),
            vmem((2, 256, 256), F32),
            vmem((2, 256, 512), F32),
            vmem((2, 16, 16, 512), F32),
            vmem((2, 128, 512), F32),
            vmem((4, 128, 128), F32),
            vmem((8, 2, 32, 128), F32),
            dma((4,)),
            dma((3,)), dma((3,)),
            dma((8,)), dma((8,)),
            dma, dma,
            dma((16,)), dma((16,)),
            dma((2, 16)), dma((2, 16)),
            dma((2, 8)), dma((2, 8)),
            dma((16,)), dma((8, 2)),
        ],
        compiler_params=pltpu.CompilerParams(
            collective_id=0, has_side_effects=True, vmem_limit_bytes=48 * 2**20
        ),
        cost_estimate=pl.CostEstimate(flops=2 * 3 * 402653184 // 2, bytes_accessed=2 * 2**20, transcendentals=0),
        name="scores",
    )(train_features, inverse, test_features)


def solution(mesh):
    placed = (P("col", "row"), P("row", "col"), P("row", "col"))
    return jax.shard_map(
        on_device, mesh=mesh, in_specs=placed, out_specs=P("col", "row"), check_vma=False
    )
```

```python
import jax
import jax.numpy as jnp
from jax import lax
from jax.experimental import pallas as pl
from jax.experimental.pallas import tpu as pltpu
from jax.sharding import PartitionSpec as P

MESH = pl.DeviceIdType.MESH
F32 = jnp.float32
BF16 = jnp.bfloat16
CHUNKS = ((0, 0), (0, 1), (1, 0), (1, 1))


def split(value):
    high = value.astype(BF16)
    return high, (value - high.astype(F32)).astype(BF16)


def dot_nt(left, right):
    def product(a, b):
        return lax.dot_general(a, b, (((1,), (1,)), ((), ())), preferred_element_type=F32)

    return product(left[0], right[1]) + product(left[1], right[0]) + product(left[0], right[0])


def device(x, yh, core, yl, z):
    return ((x * 2 + yh) * 2 + core, yl * 8 + z)


def kernel(
    x_ref, m_ref, t_ref, o_ref,
    mb, xb, ty, tb, u, rs, ag, op, fr,
    local_sem, m_send, m_recv, x_send, x_recv, ty_send, ty_recv, t_send, t_recv,
    rs_send, rs_recv, ag_send, ag_recv, f_send, f_recv,
):
    r = lax.axis_index("row")
    c = lax.axis_index("col")
    k = r % 2
    yh = (r // 2) % 2
    x = r // 4
    rp = r // 2
    yl = c // 8
    z = c % 8
    p = z % 2
    w = z // 2
    step = (1 - 2 * p) * (1 - 2 * k)

    def remote(src, dst, send, recv, to):
        return pltpu.make_async_remote_copy(
            src_ref=src, dst_ref=dst, send_sem=send, recv_sem=recv, device_id=to, device_id_type=MESH
        )

    def rows(start, size):
        return pl.ds(pl.multiple_of(start, size), size)

    sibling = device(x, yh, 1 - k, yl, z)
    across = device(x, 1 - yh, k, yl, z)

    def along_x(dx, q):
        zz = (z, (z + step) % 8, (z - step) % 8)[q]
        return device((x + dx) % 4, yh, k, yl, zz)

    def along_col(dy, dw):
        return device(x, yh, k, (yl + dy) % 4, 2 * ((w + dw) % 4) + p)

    barrier = pltpu.get_barrier_semaphore()
    greeted = [across, sibling]
    greeted += [along_x(dx, q) for dx in range(4) for q in range(3) if dx or q]
    greeted += [along_col(dy, dw) for dy in range(4) for dw in range(4) if dy or dw]
    for to in greeted:
        pl.semaphore_signal(barrier, inc=1, device_id=to, device_id_type=MESH)

    own_m = pltpu.make_async_copy(m_ref, mb.at[0, 0], local_sem.at[0])
    own_x = pltpu.make_async_copy(x_ref, xb.at[0, 0], local_sem.at[1])
    own_t = pltpu.make_async_copy(t_ref.at[rows(4 * p, 4)], tb.at[0, rows(4 * rp, 4)], local_sem.at[2])
    own_m.start()
    own_x.start()
    own_t.start()

    pl.semaphore_wait(barrier, len(greeted))

    copy_ty = remote(t_ref, ty, ty_send, ty_recv, across)
    copy_ty.start()
    t_copies = [[], [], []]

    def send_t(block_ref, b):
        to_rows = rows(4 * (2 * x + (yh if b == 0 else 1 - yh)), 4)
        for dx in (2, 1, 3, 0):
            for q in (1, 0, 2):
                if dx == 0 and q == 0:
                    continue
                half = p if q == 0 else 1 - p
                n = (b * 4 + dx) * 3 + q
                copy = remote(
                    block_ref.at[rows(4 * half, 4)], tb.at[q, to_rows],
                    t_send.at[n], t_recv.at[n], along_x(dx, q),
                )
                copy.start()
                t_copies[q].append(copy)

    send_t(t_ref, 0)
    copy_mp = remote(m_ref, mb.at[1, 0], m_send.at[0], m_recv.at[0], along_x(0, 1))
    copy_mp.start()
    copy_ms = remote(m_ref, mb.at[0, 1], m_send.at[1], m_recv.at[1], sibling)
    copy_ms.start()
    copy_ty.wait_recv()
    send_t(ty, 1)
    own_ty = pltpu.make_async_copy(
        ty.at[rows(4 * p, 4)], tb.at[0, rows(4 * (2 * x + 1 - yh), 4)], local_sem.at[3]
    )
    own_ty.start()

    x_copies = {}

    def send_x(d):
        to = device(x, yh, k, (yl + d) % 4, z)
        copy = remote(x_ref, xb.at[4 - d, 0], x_send.at[4 - d], x_recv.at[4 - d], to)
        copy.start()
        x_copies[4 - d] = copy

    send_x(1)
    send_x(3)
    copy_xs = remote(x_ref, xb.at[0, 1], x_send.at[4], x_recv.at[4], sibling)
    copy_xs.start()

    own_m.wait()
    own_t.wait()
    own_ty.wait()
    for copy in t_copies[0] + t_copies[1]:
        copy.wait_recv()
    copy_mp.wait_recv()
    copy_mr = remote(mb.at[1, 0], mb.at[1, 1], m_send.at[2], m_recv.at[2], sibling)
    copy_mr.start()

    rs_copies = []
    for ch, (tc, ic) in enumerate(CHUNKS):
        if ch == 1:
            for copy in t_copies[2]:
                copy.wait_recv()
            copy_ms.wait_recv()
            copy_mr.wait_recv()

        def test_rows(q):
            return split(tb[q].reshape(8, 2, 16, 256)[:, tc].reshape(128, 256))

        u[ch] = dot_nt(test_rows(0), split(mb[0, ic])) + dot_nt(test_rows(1 + ic), split(mb[1, ic]))
        copies = []
        for dw in (2, 1, 3, 0):
            for dy in (2, 1, 3, 0):
                e = dy * 4 + dw
                if e == 0:
                    continue
                m = 4 * ((yl + dy) % 4) + (w + dw) % 4
                copy = remote(
                    u.at[ch, rows(8 * m, 8)], rs.at[ch, e],
                    rs_send.at[ch, e], rs_recv.at[ch, e], along_col(dy, dw),
                )
                copy.start()
                copies.append(copy)
        rs_copies.append(copies)
        if ch == 1:
            send_x(2)

    mine = rows(8 * (4 * yl + w), 8)
    slot = (z // 4) * 4 + (z % 2) * 2 + (z // 2) % 2
    slot_rows = rows(8 * slot, 8)
    ag_copies = []
    relays = []
    for ch in range(4):
        for copy in rs_copies[ch]:
            copy.wait_recv()
        total = u[ch, mine]
        for e in range(1, 16):
            total = total + rs[ch, e]
        ag[ch, slot_rows] = total
        copies = []
        for dz in (4, 3, 5, 2, 6, 1, 7):
            to = device(x, yh, k, yl, (z + dz) % 8)
            copy = remote(
                ag.at[ch, slot_rows], ag.at[ch, slot_rows], ag_send.at[ch, dz], ag_recv.at[ch, dz], to
            )
            copy.start()
            copies.append(copy)
        ag_copies.append(copies)
        for d in ((), (1, 3), (2,), ())[ch]:
            x_copies[d].wait_recv()
            relay = remote(xb.at[d, 0], xb.at[d, 1], x_send.at[4 + d], x_recv.at[4 + d], sibling)
            relay.start()
            relays.append(relay)

    own_x.wait()
    copy_xs.wait_recv()
    for relay in relays:
        relay.wait_recv()

    finals = []
    for tc in range(2):
        for ch in (2 * tc, 2 * tc + 1):
            for copy in ag_copies[ch]:
                copy.wait_recv()
        a = [split(ag[2 * tc + ic]) for ic in range(2)]
        for d in range(4):
            op[tc, d] = dot_nt(a[0], split(xb[d, 0])) + dot_nt(a[1], split(xb[d, 1]))
            for g in range(2):
                for q in range(2):
                    n = ((tc * 4 + d) * 2 + g) * 2 + q
                    to = device((yl + d) % 4, z // 4, (z // 2) % 2, yl, 4 * g + 2 * k + q)
                    here = jnp.logical_and(to[0] == r, to[1] == c)
                    tile = pl.ds(16 * (2 * g + q), 16)
                    place = pl.ds(16 * tc, 16)
                    copy = remote(
                        op.at[tc, d, tile], fr.at[rp, z % 2, place],
                        f_send.at[n], f_recv.at[tc, rp, z % 2], to,
                    )
                    finals.append((here, copy))

                    @pl.when(jnp.logical_not(here))
                    def _(copy=copy):
                        copy.start()

                    @pl.when(here)
                    def _(d=d, tile=tile, place=place):
                        fr[rp, z % 2, place] = op[tc, d, tile]

    for tc in range(2):
        place = pl.ds(16 * tc, 16)
        for half in range(2):
            for s in range(8):
                z_from = 4 * yh + 2 * k + half
                here = jnp.logical_and(
                    jnp.logical_and(rp == s, z_from == z), k == (z // 2) % 2
                )
                arrival = remote(
                    op.at[0, 0, pl.ds(0, 16)], fr.at[s, half, place],
                    f_send.at[0], f_recv.at[tc, s, half], sibling,
                )

                @pl.when(jnp.logical_not(here))
                def _(arrival=arrival):
                    arrival.wait_recv()

            total = fr[0, half, place]
            for s in range(1, 8):
                total = total + fr[s, half, place]
            o_ref[place, pl.ds(128 * half, 128)] = total

    copy_ty.wait_send()
    for copies in t_copies + rs_copies + ag_copies + [relays, list(x_copies.values())]:
        for copy in copies:
            copy.wait_send()
    for copy in (copy_mp, copy_ms, copy_mr, copy_xs):
        copy.wait_send()
    for here, copy in finals:

        @pl.when(jnp.logical_not(here))
        def _(copy=copy):
            copy.wait_send()


def on_device(train_features, inverse, test_features):
    vmem = pltpu.VMEM
    dma = pltpu.SemaphoreType.DMA
    return pl.pallas_call(
        kernel,
        out_shape=jax.ShapeDtypeStruct((32, 256), F32),
        in_specs=[pl.BlockSpec(memory_space=pltpu.HBM)] * 3,
        out_specs=pl.BlockSpec(memory_space=pltpu.VMEM),
        scratch_shapes=[
            vmem((2, 2, 512, 256), F32),
            vmem((4, 2, 128, 512), F32),
            vmem((8, 8, 256), F32),
            vmem((3, 32, 8, 256), F32),
            vmem((4, 128, 512), F32),
            vmem((4, 16, 8, 512), F32),
            vmem((4, 64, 512), F32),
            vmem((2, 4, 64, 128), F32),
            vmem((8, 2, 32, 128), F32),
            dma((4,)),
            dma((3,)), dma((3,)),
            dma((8,)), dma((8,)),
            dma, dma,
            dma((24,)), dma((24,)),
            dma((4, 16)), dma((4, 16)),
            dma((4, 8)), dma((4, 8)),
            dma((32,)), dma((2, 8, 2)),
        ],
        compiler_params=pltpu.CompilerParams(
            collective_id=0, has_side_effects=True, vmem_limit_bytes=48 * 2**20
        ),
        cost_estimate=pl.CostEstimate(flops=1207959552, bytes_accessed=2 * 2**20, transcendentals=0),
        name="scores",
    )(train_features, inverse, test_features.reshape(8, 8, 256))


def solution(mesh):
    placed = (P("col", "row"), P("row", "col"), P("row", "col"))
    return jax.shard_map(
        on_device, mesh=mesh, in_specs=placed, out_specs=P("col", "row"), check_vma=False
    )
```

```python
import jax
import jax.numpy as jnp
from jax import lax
from jax.experimental import pallas as pl
from jax.experimental.pallas import tpu as pltpu
from jax.sharding import PartitionSpec as P

MESH = pl.DeviceIdType.MESH
F32 = jnp.float32
BF16 = jnp.bfloat16
CHUNKS = ((0, 0), (0, 1), (1, 0), (1, 1))


def split(value):
    high = value.astype(BF16)
    return high, (value - high.astype(F32)).astype(BF16)


def dot_nt(left, right):
    def product(a, b):
        return lax.dot_general(a, b, (((1,), (1,)), ((), ())), preferred_element_type=F32)

    return product(left[0], right[1]) + product(left[1], right[0]) + product(left[0], right[0])


def device(x, yh, core, yl, z):
    return ((x * 2 + yh) * 2 + core, yl * 8 + z)


def kernel(
    x_ref, m_ref, t_ref, o_ref,
    mb, xb, ty, tb, u, ra, sb, rb, ag, op, fr,
    local_sem, m_send, m_recv, x_send, x_recv, ty_send, ty_recv, t_send, t_recv,
    ra_send, ra_recv, rb_send, rb_recv, ag_send, ag_recv, f_send, f_recv,
):
    r = lax.axis_index("row")
    c = lax.axis_index("col")
    k = r % 2
    yh = (r // 2) % 2
    x = r // 4
    rp = r // 2
    yl = c // 8
    z = c % 8
    p = z % 2
    w = z // 2
    step = (1 - 2 * p) * (1 - 2 * k)

    def remote(src, dst, send, recv, to):
        return pltpu.make_async_remote_copy(
            src_ref=src, dst_ref=dst, send_sem=send, recv_sem=recv, device_id=to, device_id_type=MESH
        )

    def rows(start, size):
        return pl.ds(pl.multiple_of(start, size), size)

    sibling = device(x, yh, 1 - k, yl, z)
    across = device(x, 1 - yh, k, yl, z)

    def along_x(dx, q):
        zz = (z, (z + step) % 8, (z - step) % 8)[q]
        return device((x + dx) % 4, yh, k, yl, zz)

    def along_y(d):
        return device(x, yh, k, (yl + d) % 4, z)

    def along_z(d):
        return device(x, yh, k, yl, 2 * ((w + d) % 4) + p)

    barrier = pltpu.get_barrier_semaphore()
    greeted = [across, sibling]
    greeted += [along_x(dx, q) for dx in range(4) for q in range(3) if dx or q]
    greeted += [along_y(d) for d in (1, 2, 3)] + [along_z(d) for d in (1, 2, 3)]
    for to in greeted:
        pl.semaphore_signal(barrier, inc=1, device_id=to, device_id_type=MESH)

    own_m = pltpu.make_async_copy(m_ref, mb.at[0, 0], local_sem.at[0])
    own_x = pltpu.make_async_copy(x_ref, xb.at[yl, 0], local_sem.at[1])
    own_t = pltpu.make_async_copy(t_ref.at[rows(4 * p, 4)], tb.at[0, rows(4 * rp, 4)], local_sem.at[2])
    own_m.start()
    own_x.start()
    own_t.start()

    pl.semaphore_wait(barrier, len(greeted))

    copy_ty = remote(t_ref, ty, ty_send, ty_recv, across)
    copy_ty.start()
    t_copies = [[], [], []]

    def send_t(block_ref, b):
        to_rows = rows(4 * (2 * x + (yh if b == 0 else 1 - yh)), 4)
        for dx in (2, 1, 3, 0):
            for q in (1, 0, 2):
                if dx == 0 and q == 0:
                    continue
                half = p if q == 0 else 1 - p
                n = (b * 4 + dx) * 3 + q
                copy = remote(
                    block_ref.at[rows(4 * half, 4)], tb.at[q, to_rows],
                    t_send.at[n], t_recv.at[n], along_x(dx, q),
                )
                copy.start()
                t_copies[q].append(copy)

    send_t(t_ref, 0)
    copy_mp = remote(m_ref, mb.at[1, 0], m_send.at[0], m_recv.at[0], along_x(0, 1))
    copy_mp.start()
    copy_ms = remote(m_ref, mb.at[0, 1], m_send.at[1], m_recv.at[1], sibling)
    copy_ms.start()
    copy_ty.wait_recv()
    send_t(ty, 1)
    own_ty = pltpu.make_async_copy(
        ty.at[rows(4 * p, 4)], tb.at[0, rows(4 * (2 * x + 1 - yh), 4)], local_sem.at[3]
    )
    own_ty.start()

    x_hops = []

    def send_x(hop):
        for way, side in enumerate((1, -1)):
            block = yl - side * (hop - 1)
            there = yl + side
            n = 3 * way + hop - 1
            sends = jnp.logical_and(
                jnp.logical_and(block >= 0, block <= 3), jnp.logical_and(there >= 0, there <= 3)
            )
            comes = yl - side * hop
            receives = jnp.logical_and(comes >= 0, comes <= 3)
            source = x_ref if hop == 1 else xb.at[jnp.clip(block, 0, 3), 0]
            copy = remote(
                source, xb.at[jnp.clip(block, 0, 3), 0], x_send.at[n], x_recv.at[n],
                device(x, yh, k, (yl + side) % 4, z),
            )
            slot = jnp.clip(comes, 0, 3)
            relay = remote(xb.at[slot, 0], xb.at[slot, 1], x_send.at[7 + n], x_recv.at[7 + n], sibling)
            x_hops.append((sends, receives, copy, relay))

            @pl.when(sends)
            def _(copy=copy):
                copy.start()

    def pass_x(hop):
        for sends, receives, copy, relay in x_hops[2 * hop - 2:2 * hop]:

            @pl.when(receives)
            def _(copy=copy, relay=relay):
                copy.wait_recv()
                relay.start()

    send_x(1)
    copy_xs = remote(x_ref, xb.at[yl, 1], x_send.at[6], x_recv.at[6], sibling)
    copy_xs.start()

    own_m.wait()
    own_t.wait()
    own_ty.wait()
    for copy in t_copies[0] + t_copies[1]:
        copy.wait_recv()
    copy_mp.wait_recv()
    copy_mr = remote(mb.at[1, 0], mb.at[1, 1], m_send.at[2], m_recv.at[2], sibling)
    copy_mr.start()

    ra_copies = []
    for ch, (tc, ic) in enumerate(CHUNKS):
        if ch == 1:
            for copy in t_copies[2]:
                copy.wait_recv()
            copy_ms.wait_recv()
            copy_mr.wait_recv()

        def test_rows(q):
            return split(tb[q].reshape(8, 2, 16, 256)[:, tc].reshape(128, 256))

        u[ch] = (
            dot_nt(test_rows(0), split(mb[0, ic])) + dot_nt(test_rows(1 + ic), split(mb[1, ic]))
        ).reshape(4, 4, 8, 512)
        copies = []
        for d in (2, 1, 3):
            if ic == 0:
                to, part = along_z(d), u.at[ch, :, (w + d) % 4]
            else:
                to, part = along_y(d), u.at[ch, (yl + d) % 4]
            copy = remote(part, ra.at[ch, d - 1], ra_send.at[ch, d - 1], ra_recv.at[ch, d - 1], to)
            copy.start()
            copies.append(copy)
        ra_copies.append(copies)
    pass_x(1)
    send_x(2)

    rb_copies = []

    def reduce_first(ch):
        ic = CHUNKS[ch][1]
        for copy in ra_copies[ch]:
            copy.wait_recv()
        if ic == 0:
            total = u[ch, :, pl.ds(w, 1)].reshape(4, 8, 512)
        else:
            total = u[ch, pl.ds(yl, 1)].reshape(4, 8, 512)
        sb[ch] = total + ra[ch, 0] + ra[ch, 1] + ra[ch, 2]
        copies = []
        for d in (2, 1, 3):
            to, n = (along_y(d), (yl + d) % 4) if ic == 0 else (along_z(d), (w + d) % 4)
            copy = remote(sb.at[ch, n], rb.at[ch, d - 1], rb_send.at[ch, d - 1], rb_recv.at[ch, d - 1], to)
            copy.start()
            copies.append(copy)
        rb_copies.append(copies)

    slot = (z // 4) * 4 + (z % 2) * 2 + (z // 2) % 2
    slot_rows = rows(8 * slot, 8)
    ag_copies = []

    def gather(ch):
        for copy in rb_copies[ch]:
            copy.wait_recv()
        own = yl if CHUNKS[ch][1] == 0 else w
        total = sb[ch, pl.ds(own, 1)].reshape(8, 512)
        ag[ch, slot_rows] = total + rb[ch, 0] + rb[ch, 1] + rb[ch, 2]
        copies = []
        for dz in (4, 3, 5, 2, 6, 1, 7):
            to = device(x, yh, k, yl, (z + dz) % 8)
            copy = remote(
                ag.at[ch, slot_rows], ag.at[ch, slot_rows], ag_send.at[ch, dz], ag_recv.at[ch, dz], to
            )
            copy.start()
            copies.append(copy)
        ag_copies.append(copies)

    reduce_first(0)
    reduce_first(1)
    pass_x(2)
    send_x(3)
    gather(0)
    reduce_first(2)
    gather(1)
    reduce_first(3)
    gather(2)
    gather(3)
    pass_x(3)

    own_x.wait()
    copy_xs.wait_recv()
    for sends, receives, copy, relay in x_hops:

        @pl.when(receives)
        def _(relay=relay):
            relay.wait_recv()

    finals = []
    for tc in range(2):
        for ch in (2 * tc, 2 * tc + 1):
            for copy in ag_copies[ch]:
                copy.wait_recv()
        a = [split(ag[2 * tc + ic]) for ic in range(2)]
        for d in range(4):
            block = xb[pl.ds((yl + d) % 4, 1)].reshape(2, 128, 512)
            op[tc, d] = dot_nt(a[0], split(block[0])) + dot_nt(a[1], split(block[1]))
            for g in range(2):
                for q in range(2):
                    n = ((tc * 4 + d) * 2 + g) * 2 + q
                    to = device((yl + d) % 4, z // 4, (z // 2) % 2, yl, 4 * g + 2 * k + q)
                    here = jnp.logical_and(to[0] == r, to[1] == c)
                    tile = pl.ds(16 * (2 * g + q), 16)
                    place = pl.ds(16 * tc, 16)
                    copy = remote(
                        op.at[tc, d, tile], fr.at[rp, z % 2, place],
                        f_send.at[n], f_recv.at[tc, rp, z % 2], to,
                    )
                    finals.append((here, copy))

                    @pl.when(jnp.logical_not(here))
                    def _(copy=copy):
                        copy.start()

                    @pl.when(here)
                    def _(d=d, tile=tile, place=place):
                        fr[rp, z % 2, place] = op[tc, d, tile]

    for tc in range(2):
        place = pl.ds(16 * tc, 16)
        for half in range(2):
            for s in range(8):
                z_from = 4 * yh + 2 * k + half
                here = jnp.logical_and(
                    jnp.logical_and(rp == s, z_from == z), k == (z // 2) % 2
                )
                arrival = remote(
                    op.at[0, 0, pl.ds(0, 16)], fr.at[s, half, place],
                    f_send.at[0], f_recv.at[tc, s, half], sibling,
                )

                @pl.when(jnp.logical_not(here))
                def _(arrival=arrival):
                    arrival.wait_recv()

            total = fr[0, half, place]
            for s in range(1, 8):
                total = total + fr[s, half, place]
            o_ref[place, pl.ds(128 * half, 128)] = total

    copy_ty.wait_send()
    for copies in t_copies + ra_copies + rb_copies + ag_copies:
        for copy in copies:
            copy.wait_send()
    for sends, receives, copy, relay in x_hops:

        @pl.when(sends)
        def _(copy=copy):
            copy.wait_send()

        @pl.when(receives)
        def _(relay=relay):
            relay.wait_send()

    for copy in (copy_mp, copy_ms, copy_mr, copy_xs):
        copy.wait_send()
    for here, copy in finals:

        @pl.when(jnp.logical_not(here))
        def _(copy=copy):
            copy.wait_send()


def on_device(train_features, inverse, test_features):
    vmem = pltpu.VMEM
    dma = pltpu.SemaphoreType.DMA
    return pl.pallas_call(
        kernel,
        out_shape=jax.ShapeDtypeStruct((32, 256), F32),
        in_specs=[pl.BlockSpec(memory_space=pltpu.HBM)] * 3,
        out_specs=pl.BlockSpec(memory_space=pltpu.VMEM),
        scratch_shapes=[
            vmem((2, 2, 512, 256), F32),
            vmem((4, 2, 128, 512), F32),
            vmem((8, 8, 256), F32),
            vmem((3, 32, 8, 256), F32),
            vmem((4, 4, 4, 8, 512), F32),
            vmem((4, 3, 4, 8, 512), F32),
            vmem((4, 4, 8, 512), F32),
            vmem((4, 3, 8, 512), F32),
            vmem((4, 64, 512), F32),
            vmem((2, 4, 64, 128), F32),
            vmem((8, 2, 32, 128), F32),
            dma((4,)),
            dma((3,)), dma((3,)),
            dma((13,)), dma((13,)),
            dma, dma,
            dma((24,)), dma((24,)),
            dma((4, 3)), dma((4, 3)),
            dma((4, 3)), dma((4, 3)),
            dma((4, 8)), dma((4, 8)),
            dma((32,)), dma((2, 8, 2)),
        ],
        compiler_params=pltpu.CompilerParams(
            collective_id=0, has_side_effects=True, vmem_limit_bytes=64 * 2**20 - 2**16
        ),
        cost_estimate=pl.CostEstimate(flops=1207959552, bytes_accessed=2 * 2**20, transcendentals=0),
        name="scores",
    )(train_features, inverse, test_features.reshape(8, 8, 256))


def solution(mesh):
    placed = (P("col", "row"), P("row", "col"), P("row", "col"))
    return jax.shard_map(
        on_device, mesh=mesh, in_specs=placed, out_specs=P("col", "row"), check_vma=False
    )
```

```python
import jax
import jax.numpy as jnp
from jax import lax
from jax.experimental import pallas as pl
from jax.experimental.pallas import tpu as pltpu
from jax.sharding import PartitionSpec as P

MESH = pl.DeviceIdType.MESH
F32 = jnp.float32
BF16 = jnp.bfloat16
CHUNKS = ((0, 0), (0, 1), (1, 0), (1, 1))


def split(value):
    high = value.astype(BF16)
    return high, (value - high.astype(F32)).astype(BF16)


def dot_nt(left, right):
    def product(a, b):
        return lax.dot_general(a, b, (((1,), (1,)), ((), ())), preferred_element_type=F32)

    return product(left[0], right[1]) + product(left[1], right[0]) + product(left[0], right[0])


def device(x, yh, core, yl, z):
    return ((x * 2 + yh) * 2 + core, yl * 8 + z)


def kernel(
    x_ref, m_ref, t_ref, o_ref,
    mb, xb, ty, tb, u, ra, sb, rb, ag, op, fa, fs, fr,
    local_sem, m_send, m_recv, x_send, x_recv, ty_send, ty_recv, t_send, t_recv,
    ra_send, ra_recv, rb_send, rb_recv, ag_send, ag_recv, fa_send, fa_recv, f_send, f_recv,
):
    r = lax.axis_index("row")
    c = lax.axis_index("col")
    k = r % 2
    yh = (r // 2) % 2
    x = r // 4
    rp = r // 2
    yl = c // 8
    z = c % 8
    p = z % 2
    w = z // 2
    step = (1 - 2 * p) * (1 - 2 * k)

    def remote(src, dst, send, recv, to):
        return pltpu.make_async_remote_copy(
            src_ref=src, dst_ref=dst, send_sem=send, recv_sem=recv, device_id=to, device_id_type=MESH
        )

    def rows(start, size):
        return pl.ds(pl.multiple_of(start, size), size)

    sibling = device(x, yh, 1 - k, yl, z)
    across = device(x, 1 - yh, k, yl, z)

    def along_x(dx, q):
        zz = (z, (z + step) % 8, (z - step) % 8)[q]
        return device((x + dx) % 4, yh, k, yl, zz)

    def along_y(d):
        return device(x, yh, k, (yl + d) % 4, z)

    def along_z(d):
        return device(x, yh, k, yl, 2 * ((w + d) % 4) + p)

    barrier = pltpu.get_barrier_semaphore()
    greeted = [across, sibling]
    greeted += [along_x(dx, q) for dx in range(4) for q in range(3) if dx or q]
    greeted += [along_y(d) for d in (1, 2, 3)] + [along_z(d) for d in (1, 2, 3)]
    for to in greeted:
        pl.semaphore_signal(barrier, inc=1, device_id=to, device_id_type=MESH)

    own_m = pltpu.make_async_copy(m_ref, mb.at[0, 0], local_sem.at[0])
    own_x = pltpu.make_async_copy(x_ref, xb.at[yl, 0], local_sem.at[1])
    own_t = pltpu.make_async_copy(t_ref.at[rows(4 * p, 4)], tb.at[0, rows(4 * rp, 4)], local_sem.at[2])
    own_m.start()
    own_x.start()
    own_t.start()

    pl.semaphore_wait(barrier, len(greeted))

    copy_ty = remote(t_ref, ty, ty_send, ty_recv, across)
    copy_ty.start()
    x_hops = []

    def send_x(hop):
        for way, side in enumerate((1, -1)):
            block = yl - side * (hop - 1)
            there = yl + side
            n = 3 * way + hop - 1
            sends = jnp.logical_and(
                jnp.logical_and(block >= 0, block <= 3), jnp.logical_and(there >= 0, there <= 3)
            )
            comes = yl - side * hop
            receives = jnp.logical_and(comes >= 0, comes <= 3)
            source = x_ref if hop == 1 else xb.at[jnp.clip(block, 0, 3), 0]
            copy = remote(
                source, xb.at[jnp.clip(block, 0, 3), 0], x_send.at[n], x_recv.at[n],
                device(x, yh, k, (yl + side) % 4, z),
            )
            slot = jnp.clip(comes, 0, 3)
            relay = remote(xb.at[slot, 0], xb.at[slot, 1], x_send.at[7 + n], x_recv.at[7 + n], sibling)
            x_hops.append((sends, receives, copy, relay))

            @pl.when(sends)
            def _(copy=copy):
                copy.start()

    def pass_x(hop):
        for sends, receives, copy, relay in x_hops[2 * hop - 2:2 * hop]:

            @pl.when(receives)
            def _(copy=copy, relay=relay):
                copy.wait_recv()
                relay.start()

    send_x(1)
    copy_xs = remote(x_ref, xb.at[yl, 1], x_send.at[6], x_recv.at[6], sibling)
    copy_xs.start()

    t_copies = [[], [], []]

    def send_t(block_ref, b):
        to_rows = rows(4 * (2 * x + (yh if b == 0 else 1 - yh)), 4)
        for dx in (2, 1, 3, 0):
            for q in (1, 0, 2):
                if dx == 0 and q == 0:
                    continue
                half = p if q == 0 else 1 - p
                n = (b * 4 + dx) * 3 + q
                copy = remote(
                    block_ref.at[rows(4 * half, 4)], tb.at[q, to_rows],
                    t_send.at[n], t_recv.at[n], along_x(dx, q),
                )
                copy.start()
                t_copies[q].append(copy)

    send_t(t_ref, 0)
    copy_mp = remote(m_ref, mb.at[1, 0], m_send.at[0], m_recv.at[0], along_x(0, 1))
    copy_mp.start()
    copy_ms = remote(m_ref, mb.at[0, 1], m_send.at[1], m_recv.at[1], sibling)
    copy_ms.start()
    copy_ty.wait_recv()
    send_t(ty, 1)
    own_ty = pltpu.make_async_copy(
        ty.at[rows(4 * p, 4)], tb.at[0, rows(4 * (2 * x + 1 - yh), 4)], local_sem.at[3]
    )
    own_ty.start()

    own_m.wait()
    own_t.wait()
    own_ty.wait()
    for copy in t_copies[0] + t_copies[1]:
        copy.wait_recv()
    copy_mp.wait_recv()
    copy_mr = remote(mb.at[1, 0], mb.at[1, 1], m_send.at[2], m_recv.at[2], sibling)
    copy_mr.start()

    pass_x(1)
    send_x(2)
    ra_copies = []
    for ch, (tc, ic) in enumerate(CHUNKS):
        if ch == 1:
            for copy in t_copies[2]:
                copy.wait_recv()
            copy_ms.wait_recv()
            copy_mr.wait_recv()

        def test_rows(q):
            return split(tb[q].reshape(8, 2, 16, 256)[:, tc].reshape(128, 256))

        u[ch] = (
            dot_nt(test_rows(0), split(mb[0, ic])) + dot_nt(test_rows(1 + ic), split(mb[1, ic]))
        ).reshape(4, 4, 8, 512)
        copies = []
        if ch >= 2:
            for copy in ra_copies[ch - 2]:
                copy.wait_send()
        for d in (2, 1, 3):
            if ic == 0:
                to, part = along_z(d), u.at[ch, :, (w + d) % 4]
            else:
                to, part = along_y(d), u.at[ch, (yl + d) % 4]
            copy = remote(part, ra.at[ch, d - 1], ra_send.at[ch, d - 1], ra_recv.at[ch, d - 1], to)
            copy.start()
            copies.append(copy)
        ra_copies.append(copies)

    rb_copies = []

    def reduce_first(ch):
        ic = CHUNKS[ch][1]
        for copy in ra_copies[ch]:
            copy.wait_recv()
        if ic == 0:
            total = u[ch, :, pl.ds(w, 1)].reshape(4, 8, 512)
        else:
            total = u[ch, pl.ds(yl, 1)].reshape(4, 8, 512)
        sb[ch] = total + ra[ch, 0] + ra[ch, 1] + ra[ch, 2]
        copies = []
        for d in (2, 1, 3):
            to, n = (along_y(d), (yl + d) % 4) if ic == 0 else (along_z(d), (w + d) % 4)
            copy = remote(sb.at[ch, n], rb.at[ch, d - 1], rb_send.at[ch, d - 1], rb_recv.at[ch, d - 1], to)
            copy.start()
            copies.append(copy)
        rb_copies.append(copies)

    slot = (z // 4) * 4 + (z % 2) * 2 + (z // 2) % 2
    slot_rows = rows(8 * slot, 8)
    ag_copies = []

    def gather(ch):
        for copy in rb_copies[ch]:
            copy.wait_recv()
        own = yl if CHUNKS[ch][1] == 0 else w
        total = sb[ch, pl.ds(own, 1)].reshape(8, 512)
        ag[ch, slot_rows] = total + rb[ch, 0] + rb[ch, 1] + rb[ch, 2]
        copies = []
        for dz in (4, 3, 5, 2, 6, 1, 7):
            to = device(x, yh, k, yl, (z + dz) % 8)
            copy = remote(
                ag.at[ch, slot_rows], ag.at[ch, slot_rows], ag_send.at[ch, dz], ag_recv.at[ch, dz], to
            )
            copy.start()
            copies.append(copy)
        ag_copies.append(copies)

    reduce_first(0)
    reduce_first(1)
    pass_x(2)
    send_x(3)
    gather(0)
    reduce_first(2)
    gather(1)
    reduce_first(3)
    gather(2)
    gather(3)
    pass_x(3)

    own_x.wait()
    copy_xs.wait_recv()
    for sends, receives, copy, relay in x_hops:

        @pl.when(receives)
        def _(relay=relay):
            relay.wait_recv()

    finals = []
    fa_copies = []
    for tc in range(2):
        for ch in (2 * tc, 2 * tc + 1):
            for copy in ag_copies[ch]:
                copy.wait_recv()
        a = [split(ag[2 * tc + ic]) for ic in range(2)]
        copies = []
        for dx in (2, 1, 3, 0):
            block = xb[pl.ds((x + dx) % 4, 1)].reshape(2, 128, 512)
            op[tc, dx] = dot_nt(a[0], split(block[0])) + dot_nt(a[1], split(block[1]))
            if dx:
                copy = remote(
                    op.at[tc, dx], fa.at[tc, dx - 1],
                    fa_send.at[tc, dx - 1], fa_recv.at[tc, dx - 1], along_x(dx, 0),
                )
                copy.start()
                copies.append(copy)
        fa_copies.append(copies)

    core_out = (z // 2) % 2
    for tc in range(2):
        for copy in fa_copies[tc]:
            copy.wait_recv()
        fs[tc] = op[tc, 0] + fa[tc, 0] + fa[tc, 1] + fa[tc, 2]
        place = pl.ds(16 * tc, 16)
        for g in range(2):
            for q in range(2):
                n = 2 * g + q
                z_out = 4 * g + 2 * k + q
                here = jnp.logical_and(
                    jnp.logical_and(yh == z // 4, k == core_out), z == z_out
                )
                tile = pl.ds(16 * n, 16)
                copy = remote(
                    fs.at[tc, tile], fr.at[yh, z % 2, place],
                    f_send.at[tc, n], f_recv.at[tc, yh, z % 2],
                    device(x, z // 4, core_out, yl, z_out),
                )
                finals.append((here, copy))

                @pl.when(jnp.logical_not(here))
                def _(copy=copy):
                    copy.start()

                @pl.when(here)
                def _(tc=tc, tile=tile, place=place):
                    fr[yh, z % 2, place] = fs[tc, tile]

    for tc in range(2):
        place = pl.ds(16 * tc, 16)
        for half in range(2):
            for s in range(2):
                here = jnp.logical_and(
                    jnp.logical_and(yh == s, 4 * yh + 2 * k + half == z), k == core_out
                )
                arrival = remote(
                    fs.at[0, pl.ds(0, 16)], fr.at[s, half, place],
                    f_send.at[0, 0], f_recv.at[tc, s, half], sibling,
                )

                @pl.when(jnp.logical_not(here))
                def _(arrival=arrival):
                    arrival.wait_recv()

            o_ref[place, pl.ds(128 * half, 128)] = fr[0, half, place] + fr[1, half, place]

    copy_ty.wait_send()
    for copies in t_copies + ra_copies[2:] + rb_copies + ag_copies + fa_copies:
        for copy in copies:
            copy.wait_send()
    for sends, receives, copy, relay in x_hops:

        @pl.when(sends)
        def _(copy=copy):
            copy.wait_send()

        @pl.when(receives)
        def _(relay=relay):
            relay.wait_send()

    for copy in (copy_mp, copy_ms, copy_mr, copy_xs):
        copy.wait_send()
    for here, copy in finals:

        @pl.when(jnp.logical_not(here))
        def _(copy=copy):
            copy.wait_send()


def on_device(train_features, inverse, test_features):
    vmem = pltpu.VMEM
    dma = pltpu.SemaphoreType.DMA
    return pl.pallas_call(
        kernel,
        out_shape=jax.ShapeDtypeStruct((32, 256), F32),
        in_specs=[pl.BlockSpec(memory_space=pltpu.HBM)] * 3,
        out_specs=pl.BlockSpec(memory_space=pltpu.VMEM),
        scratch_shapes=[
            vmem((2, 2, 512, 256), F32),
            vmem((4, 2, 128, 512), F32),
            vmem((8, 8, 256), F32),
            vmem((3, 32, 8, 256), F32),
            vmem((4, 4, 4, 8, 512), F32),
            vmem((4, 3, 4, 8, 512), F32),
            vmem((4, 4, 8, 512), F32),
            vmem((4, 3, 8, 512), F32),
            vmem((4, 64, 512), F32),
            vmem((2, 4, 64, 128), F32),
            vmem((2, 3, 64, 128), F32),
            vmem((2, 64, 128), F32),
            vmem((2, 2, 32, 128), F32),
            dma((4,)),
            dma((3,)), dma((3,)),
            dma((13,)), dma((13,)),
            dma, dma,
            dma((24,)), dma((24,)),
            dma((4, 3)), dma((4, 3)),
            dma((4, 3)), dma((4, 3)),
            dma((4, 8)), dma((4, 8)),
            dma((2, 3)), dma((2, 3)),
            dma((2, 4)), dma((2, 2, 2)),
        ],
        compiler_params=pltpu.CompilerParams(
            collective_id=0, has_side_effects=True, vmem_limit_bytes=64 * 2**20 - 2**16
        ),
        cost_estimate=pl.CostEstimate(flops=1207959552, bytes_accessed=2 * 2**20, transcendentals=0),
        name="scores",
    )(train_features, inverse, test_features.reshape(8, 8, 256))


def solution(mesh):
    placed = (P("col", "row"), P("row", "col"), P("row", "col"))
    return jax.shard_map(
        on_device, mesh=mesh, in_specs=placed, out_specs=P("col", "row"), check_vma=False
    )
```

```python
import jax
import jax.numpy as jnp
from jax import lax
from jax.experimental import pallas as pl
from jax.experimental.pallas import tpu as pltpu
from jax.sharding import PartitionSpec as P

MESH = pl.DeviceIdType.MESH
F32 = jnp.float32
BF16 = jnp.bfloat16
AX = (0, 0, 1, 0)
CHUNKS = ((0, 0), (0, 1), (1, 0), (1, 1))


def split(value):
    high = value.astype(BF16)
    return high, (value - high.astype(F32)).astype(BF16)


def dot_nt(left, right):
    def product(a, b):
        return lax.dot_general(a, b, (((1,), (1,)), ((), ())), preferred_element_type=F32)

    return product(left[0], right[1]) + product(left[1], right[0]) + product(left[0], right[0])


def device(x, yh, core, yl, z):
    return ((x * 2 + yh) * 2 + core, yl * 8 + z)


def kernel(
    x_ref, m_ref, t_ref, o_ref,
    mb, xb, ty, tb, u, ra, sb, rb, ag, op, fa, fs, fr,
    local_sem, m_send, m_recv, x_send, x_recv, ty_send, ty_recv, t_send, t_recv,
    ra_send, ra_recv, rb_send, rb_recv, ag_send, ag_recv, fa_send, fa_recv, f_send, f_recv,
):
    r = lax.axis_index("row")
    c = lax.axis_index("col")
    k = r % 2
    yh = (r // 2) % 2
    x = r // 4
    rp = r // 2
    yl = c // 8
    z = c % 8
    p = z % 2
    w = z // 2
    step = (1 - 2 * p) * (1 - 2 * k)

    def remote(src, dst, send, recv, to):
        return pltpu.make_async_remote_copy(
            src_ref=src, dst_ref=dst, send_sem=send, recv_sem=recv, device_id=to, device_id_type=MESH
        )

    def rows(start, size):
        return pl.ds(pl.multiple_of(start, size), size)

    sibling = device(x, yh, 1 - k, yl, z)
    across = device(x, 1 - yh, k, yl, z)

    def along_x(dx, q):
        zz = (z, (z + step) % 8, (z - step) % 8)[q]
        return device((x + dx) % 4, yh, k, yl, zz)

    def along_y(d):
        return device(x, yh, k, (yl + d) % 4, z)

    def along_z(d):
        return device(x, yh, k, yl, 2 * ((w + d) % 4) + p)

    barrier = pltpu.get_barrier_semaphore()
    greeted = [across, sibling]
    greeted += [along_x(dx, q) for dx in range(4) for q in range(3) if dx or q]
    greeted += [along_y(d) for d in (1, 2, 3)] + [along_z(d) for d in (1, 2, 3)]
    for to in greeted:
        pl.semaphore_signal(barrier, inc=1, device_id=to, device_id_type=MESH)

    own_m = pltpu.make_async_copy(m_ref, mb.at[0, 0], local_sem.at[0])
    own_x = pltpu.make_async_copy(x_ref, xb.at[yl, 0], local_sem.at[1])
    own_t = pltpu.make_async_copy(t_ref.at[rows(4 * p, 4)], tb.at[0, rows(4 * rp, 4)], local_sem.at[2])
    own_m.start()
    own_x.start()
    own_t.start()

    pl.semaphore_wait(barrier, len(greeted))

    copy_ty = remote(t_ref, ty, ty_send, ty_recv, across)
    copy_ty.start()
    x_hops = []

    def send_x(hop):
        for way, side in enumerate((1, -1)):
            block = yl - side * (hop - 1)
            there = yl + side
            n = 3 * way + hop - 1
            sends = jnp.logical_and(
                jnp.logical_and(block >= 0, block <= 3), jnp.logical_and(there >= 0, there <= 3)
            )
            comes = yl - side * hop
            receives = jnp.logical_and(comes >= 0, comes <= 3)
            source = x_ref if hop == 1 else xb.at[jnp.clip(block, 0, 3), 0]
            copy = remote(
                source, xb.at[jnp.clip(block, 0, 3), 0], x_send.at[n], x_recv.at[n],
                device(x, yh, k, (yl + side) % 4, z),
            )
            slot = jnp.clip(comes, 0, 3)
            relay = remote(xb.at[slot, 0], xb.at[slot, 1], x_send.at[7 + n], x_recv.at[7 + n], sibling)
            x_hops.append((sends, receives, copy, relay))

            @pl.when(sends)
            def _(copy=copy):
                copy.start()

    def pass_x(hop):
        for sends, receives, copy, relay in x_hops[2 * hop - 2:2 * hop]:

            @pl.when(receives)
            def _(copy=copy, relay=relay):
                copy.wait_recv()
                relay.start()

    send_x(1)
    copy_xs = remote(x_ref, xb.at[yl, 1], x_send.at[6], x_recv.at[6], sibling)
    copy_xs.start()

    t_copies = [[], [], []]

    def send_t(block_ref, b):
        to_rows = rows(4 * (2 * x + (yh if b == 0 else 1 - yh)), 4)
        for dx in (2, 1, 3, 0):
            for q in (1, 0, 2):
                if dx == 0 and q == 0:
                    continue
                half = p if q == 0 else 1 - p
                n = (b * 4 + dx) * 3 + q
                copy = remote(
                    block_ref.at[rows(4 * half, 4)], tb.at[q, to_rows],
                    t_send.at[n], t_recv.at[n], along_x(dx, q),
                )
                copy.start()
                t_copies[q].append(copy)

    copy_mp = remote(m_ref, mb.at[1, 0], m_send.at[0], m_recv.at[0], along_x(0, 1))
    copy_mp.start()
    send_t(t_ref, 0)
    copy_ms = remote(m_ref, mb.at[0, 1], m_send.at[1], m_recv.at[1], sibling)
    copy_ms.start()
    copy_ty.wait_recv()
    send_t(ty, 1)
    own_ty = pltpu.make_async_copy(
        ty.at[rows(4 * p, 4)], tb.at[0, rows(4 * (2 * x + 1 - yh), 4)], local_sem.at[3]
    )
    own_ty.start()

    pass_x(1)
    send_x(2)
    own_m.wait()
    own_t.wait()
    own_ty.wait()
    for copy in t_copies[0] + t_copies[1]:
        copy.wait_recv()
    copy_mp.wait_recv()
    copy_mr = remote(mb.at[1, 0], mb.at[1, 1], m_send.at[2], m_recv.at[2], sibling)
    copy_mr.start()

    ra_copies = []
    for ch, (tc, ic) in enumerate(CHUNKS):
        if ch == 1:
            for copy in t_copies[2]:
                copy.wait_recv()
            copy_ms.wait_recv()
            copy_mr.wait_recv()

        def test_rows(q):
            return split(tb[q].reshape(8, 2, 16, 256)[:, tc].reshape(128, 256))

        u[ch] = (
            dot_nt(test_rows(0), split(mb[0, ic])) + dot_nt(test_rows(1 + ic), split(mb[1, ic]))
        ).reshape(4, 4, 8, 512)
        copies = []
        for d in (2, 1, 3):
            if AX[ch] == 0:
                to, part = along_z(d), u.at[ch, :, (w + d) % 4]
            else:
                to, part = along_y(d), u.at[ch, (yl + d) % 4]
            copy = remote(part, ra.at[ch, d - 1], ra_send.at[ch, d - 1], ra_recv.at[ch, d - 1], to)
            copy.start()
            copies.append(copy)
        ra_copies.append(copies)

    rb_copies = []

    def reduce_first(ch):
        ic = CHUNKS[ch][1]
        for copy in ra_copies[ch]:
            copy.wait_recv()
        if AX[ch] == 0:
            total = u[ch, :, pl.ds(w, 1)].reshape(4, 8, 512)
        else:
            total = u[ch, pl.ds(yl, 1)].reshape(4, 8, 512)
        sb[ch] = total + ra[ch, 0] + ra[ch, 1] + ra[ch, 2]
        copies = []
        for d in (2, 1, 3):
            to, n = (along_y(d), (yl + d) % 4) if AX[ch] == 0 else (along_z(d), (w + d) % 4)
            copy = remote(sb.at[ch, n], rb.at[ch, d - 1], rb_send.at[ch, d - 1], rb_recv.at[ch, d - 1], to)
            copy.start()
            copies.append(copy)
        rb_copies.append(copies)

    slot = (z // 4) * 4 + (z % 2) * 2 + (z // 2) % 2
    slot_rows = rows(8 * slot, 8)
    ag_copies = []

    def gather(ch):
        for copy in rb_copies[ch]:
            copy.wait_recv()
        own = yl if AX[ch] == 0 else w
        total = sb[ch, pl.ds(own, 1)].reshape(8, 512)
        ag[ch, slot_rows] = total + rb[ch, 0] + rb[ch, 1] + rb[ch, 2]
        copies = []
        for dz in (4, 3, 5, 2, 6, 1, 7):
            to = device(x, yh, k, yl, (z + dz) % 8)
            copy = remote(
                ag.at[ch, slot_rows], ag.at[ch, slot_rows], ag_send.at[ch, dz], ag_recv.at[ch, dz], to
            )
            copy.start()
            copies.append(copy)
        ag_copies.append(copies)

    reduce_first(0)
    reduce_first(1)
    pass_x(2)
    send_x(3)
    gather(0)
    reduce_first(2)
    gather(1)
    reduce_first(3)
    gather(2)
    gather(3)
    pass_x(3)

    own_x.wait()
    copy_xs.wait_recv()
    for sends, receives, copy, relay in x_hops:

        @pl.when(receives)
        def _(relay=relay):
            relay.wait_recv()

    finals = []
    fa_copies = []
    for tc in range(2):
        for ch in (2 * tc, 2 * tc + 1):
            for copy in ag_copies[ch]:
                copy.wait_recv()
        a = [split(ag[2 * tc + ic]) for ic in range(2)]
        copies = []
        for dx in (2, 1, 3, 0):
            block = xb[pl.ds((x + dx) % 4, 1)].reshape(2, 128, 512)
            op[tc, dx] = dot_nt(a[0], split(block[0])) + dot_nt(a[1], split(block[1]))
            if dx:
                copy = remote(
                    op.at[tc, dx], fa.at[tc, dx - 1],
                    fa_send.at[tc, dx - 1], fa_recv.at[tc, dx - 1], along_x(dx, 0),
                )
                copy.start()
                copies.append(copy)
        fa_copies.append(copies)

    core_out = (z // 2) % 2
    for tc in range(2):
        for copy in fa_copies[tc]:
            copy.wait_recv()
        fs[tc] = op[tc, 0] + fa[tc, 0] + fa[tc, 1] + fa[tc, 2]
        place = pl.ds(16 * tc, 16)
        for g in range(2):
            for q in range(2):
                n = 2 * g + q
                z_out = 4 * g + 2 * k + q
                here = jnp.logical_and(
                    jnp.logical_and(yh == z // 4, k == core_out), z == z_out
                )
                tile = pl.ds(16 * n, 16)
                copy = remote(
                    fs.at[tc, tile], fr.at[yh, z % 2, place],
                    f_send.at[tc, n], f_recv.at[tc, yh, z % 2],
                    device(x, z // 4, core_out, yl, z_out),
                )
                finals.append((here, copy))

                @pl.when(jnp.logical_not(here))
                def _(copy=copy):
                    copy.start()

                @pl.when(here)
                def _(tc=tc, tile=tile, place=place):
                    fr[yh, z % 2, place] = fs[tc, tile]

    for tc in range(2):
        place = pl.ds(16 * tc, 16)
        for half in range(2):
            for s in range(2):
                here = jnp.logical_and(
                    jnp.logical_and(yh == s, 4 * yh + 2 * k + half == z), k == core_out
                )
                arrival = remote(
                    fs.at[0, pl.ds(0, 16)], fr.at[s, half, place],
                    f_send.at[0, 0], f_recv.at[tc, s, half], sibling,
                )

                @pl.when(jnp.logical_not(here))
                def _(arrival=arrival):
                    arrival.wait_recv()

            o_ref[place, pl.ds(128 * half, 128)] = fr[0, half, place] + fr[1, half, place]

    copy_ty.wait_send()
    for copies in t_copies + ra_copies + rb_copies + ag_copies + fa_copies:
        for copy in copies:
            copy.wait_send()
    for sends, receives, copy, relay in x_hops:

        @pl.when(sends)
        def _(copy=copy):
            copy.wait_send()

        @pl.when(receives)
        def _(relay=relay):
            relay.wait_send()

    for copy in (copy_mp, copy_ms, copy_mr, copy_xs):
        copy.wait_send()
    for here, copy in finals:

        @pl.when(jnp.logical_not(here))
        def _(copy=copy):
            copy.wait_send()


def on_device(train_features, inverse, test_features):
    vmem = pltpu.VMEM
    dma = pltpu.SemaphoreType.DMA
    return pl.pallas_call(
        kernel,
        out_shape=jax.ShapeDtypeStruct((32, 256), F32),
        in_specs=[pl.BlockSpec(memory_space=pltpu.HBM)] * 3,
        out_specs=pl.BlockSpec(memory_space=pltpu.VMEM),
        scratch_shapes=[
            vmem((2, 2, 512, 256), F32),
            vmem((4, 2, 128, 512), F32),
            vmem((8, 8, 256), F32),
            vmem((3, 32, 8, 256), F32),
            vmem((4, 4, 4, 8, 512), F32),
            vmem((4, 3, 4, 8, 512), F32),
            vmem((4, 4, 8, 512), F32),
            vmem((4, 3, 8, 512), F32),
            vmem((4, 64, 512), F32),
            vmem((2, 4, 64, 128), F32),
            vmem((2, 3, 64, 128), F32),
            vmem((2, 64, 128), F32),
            vmem((2, 2, 32, 128), F32),
            dma((4,)),
            dma((3,)), dma((3,)),
            dma((13,)), dma((13,)),
            dma, dma,
            dma((24,)), dma((24,)),
            dma((4, 3)), dma((4, 3)),
            dma((4, 3)), dma((4, 3)),
            dma((4, 8)), dma((4, 8)),
            dma((2, 3)), dma((2, 3)),
            dma((2, 4)), dma((2, 2, 2)),
        ],
        compiler_params=pltpu.CompilerParams(
            collective_id=0, has_side_effects=True, vmem_limit_bytes=64 * 2**20 - 2**16
        ),
        cost_estimate=pl.CostEstimate(flops=1207959552, bytes_accessed=2 * 2**20, transcendentals=0),
        name="scores",
    )(train_features, inverse, test_features.reshape(8, 8, 256))


def solution(mesh):
    placed = (P("col", "row"), P("row", "col"), P("row", "col"))
    return jax.shard_map(
        on_device, mesh=mesh, in_specs=placed, out_specs=P("col", "row"), check_vma=False
    )
```

```python
import jax
import jax.numpy as jnp
from jax import lax
from jax.experimental import pallas as pl
from jax.experimental.pallas import tpu as pltpu
from jax.sharding import PartitionSpec as P

MESH = pl.DeviceIdType.MESH
F32 = jnp.float32
BF16 = jnp.bfloat16
AX = (0, 0, 1, 0)
CHUNKS = ((0, 0), (0, 1), (1, 0), (1, 1))


def split(value):
    high = value.astype(BF16)
    return high, (value - high.astype(F32)).astype(BF16)


def dot_nt(left, right):
    def product(a, b):
        return lax.dot_general(a, b, (((1,), (1,)), ((), ())), preferred_element_type=F32)

    return product(left[0], right[1]) + product(left[1], right[0]) + product(left[0], right[0])


def device(x, yh, core, yl, z):
    return ((x * 2 + yh) * 2 + core, yl * 8 + z)


def kernel(
    x_ref, m_ref, t_ref, o_ref,
    mb, ms, xb, xs, ty, tb, u, ra, sb, rb, ag, op, fa, fs, fr,
    local_sem, m_send, m_recv, x_send, x_recv, ty_send, ty_recv, t_send, t_recv,
    ra_send, ra_recv, rb_send, rb_recv, ag_send, ag_recv, fa_send, fa_recv, f_send, f_recv,
):
    r = lax.axis_index("row")
    c = lax.axis_index("col")
    k = r % 2
    yh = (r // 2) % 2
    x = r // 4
    rp = r // 2
    yl = c // 8
    z = c % 8
    p = z % 2
    w = z // 2
    step = (1 - 2 * p) * (1 - 2 * k)

    def remote(src, dst, send, recv, to):
        return pltpu.make_async_remote_copy(
            src_ref=src, dst_ref=dst, send_sem=send, recv_sem=recv, device_id=to, device_id_type=MESH
        )

    def rows(start, size):
        return pl.ds(pl.multiple_of(start, size), size)

    sibling = device(x, yh, 1 - k, yl, z)
    across = device(x, 1 - yh, k, yl, z)

    def along_x(dx, q):
        zz = (z, (z + step) % 8, (z - step) % 8)[q]
        return device((x + dx) % 4, yh, k, yl, zz)

    def along_y(d):
        return device(x, yh, k, (yl + d) % 4, z)

    def along_z(d):
        return device(x, yh, k, yl, 2 * ((w + d) % 4) + p)

    barrier = pltpu.get_barrier_semaphore()
    greeted = [across, sibling]
    greeted += [along_x(dx, q) for dx in range(4) for q in range(3) if dx or q]
    greeted += [along_y(d) for d in (1, 2, 3)] + [along_z(d) for d in (1, 2, 3)]
    for to in greeted:
        pl.semaphore_signal(barrier, inc=1, device_id=to, device_id_type=MESH)

    own_m = pltpu.make_async_copy(m_ref, mb.at[0, 0], local_sem.at[0])
    own_x = pltpu.make_async_copy(x_ref, xb.at[yl, 0], local_sem.at[1])
    own_t = pltpu.make_async_copy(t_ref.at[rows(4 * p, 4)], tb.at[0, rows(4 * rp, 4)], local_sem.at[2])
    own_m.start()
    own_x.start()
    own_t.start()

    pl.semaphore_wait(barrier, len(greeted))

    copy_ty = remote(t_ref, ty, ty_send, ty_recv, across)
    copy_ty.start()
    x_hops = []

    def send_x(hop):
        for way, side in enumerate((1, -1)):
            block = yl - side * (hop - 1)
            there = yl + side
            n = 3 * way + hop - 1
            sends = jnp.logical_and(
                jnp.logical_and(block >= 0, block <= 3), jnp.logical_and(there >= 0, there <= 3)
            )
            comes = yl - side * hop
            receives = jnp.logical_and(comes >= 0, comes <= 3)
            source = x_ref if hop == 1 else xb.at[jnp.clip(block, 0, 3), 0]
            copy = remote(
                source, xb.at[jnp.clip(block, 0, 3), 0], x_send.at[n], x_recv.at[n],
                device(x, yh, k, (yl + side) % 4, z),
            )
            slot = jnp.clip(comes, 0, 3)
            relay = remote(xb.at[slot, 0], xb.at[slot, 1], x_send.at[7 + n], x_recv.at[7 + n], sibling)
            x_hops.append((sends, receives, copy, relay))

            @pl.when(sends)
            def _(copy=copy):
                copy.start()

    def pass_x(hop):
        for sends, receives, copy, relay in x_hops[2 * hop - 2:2 * hop]:

            @pl.when(receives)
            def _(copy=copy, relay=relay):
                copy.wait_recv()
                relay.start()

    send_x(1)
    copy_xs = remote(x_ref, xb.at[yl, 1], x_send.at[6], x_recv.at[6], sibling)
    copy_xs.start()

    t_copies = [[], [], []]

    def send_t(block_ref, b):
        to_rows = rows(4 * (2 * x + (yh if b == 0 else 1 - yh)), 4)
        for dx in (2, 1, 3, 0):
            for q in (1, 0, 2):
                if dx == 0 and q == 0:
                    continue
                half = p if q == 0 else 1 - p
                n = (b * 4 + dx) * 3 + q
                copy = remote(
                    block_ref.at[rows(4 * half, 4)], tb.at[q, to_rows],
                    t_send.at[n], t_recv.at[n], along_x(dx, q),
                )
                copy.start()
                t_copies[q].append(copy)

    copy_mp = remote(m_ref, mb.at[1, 0], m_send.at[0], m_recv.at[0], along_x(0, 1))
    copy_mp.start()
    send_t(t_ref, 0)
    copy_ms = remote(m_ref, mb.at[0, 1], m_send.at[1], m_recv.at[1], sibling)
    copy_ms.start()
    copy_ty.wait_recv()
    send_t(ty, 1)
    own_ty = pltpu.make_async_copy(
        ty.at[rows(4 * p, 4)], tb.at[0, rows(4 * (2 * x + 1 - yh), 4)], local_sem.at[3]
    )
    own_ty.start()

    pass_x(1)
    send_x(2)
    made = set()

    def inverse_halves(j, ic):
        if (j, ic) not in made:
            made.add((j, ic))
            ms[0, j, ic], ms[1, j, ic] = split(mb[j, ic])
        return ms[0, j, ic], ms[1, j, ic]

    own_m.wait()
    inverse_halves(0, 0)
    copy_ms.wait_recv()
    inverse_halves(0, 1)

    own_t.wait()
    own_ty.wait()
    for copy in t_copies[0] + t_copies[1]:
        copy.wait_recv()
    copy_mp.wait_recv()
    copy_mr = remote(mb.at[1, 0], mb.at[1, 1], m_send.at[2], m_recv.at[2], sibling)
    copy_mr.start()

    ra_copies = []
    for ch, (tc, ic) in enumerate(CHUNKS):
        if ch == 1:
            for copy in t_copies[2]:
                copy.wait_recv()
            copy_mr.wait_recv()

        def test_rows(q):
            return split(tb[q].reshape(8, 2, 16, 256)[:, tc].reshape(128, 256))

        u[ch] = (
            dot_nt(test_rows(0), inverse_halves(0, ic)) + dot_nt(test_rows(1 + ic), inverse_halves(1, ic))
        ).reshape(4, 4, 8, 512)
        copies = []
        for d in (2, 1, 3):
            if AX[ch] == 0:
                to, part = along_z(d), u.at[ch, :, (w + d) % 4]
            else:
                to, part = along_y(d), u.at[ch, (yl + d) % 4]
            copy = remote(part, ra.at[ch, d - 1], ra_send.at[ch, d - 1], ra_recv.at[ch, d - 1], to)
            copy.start()
            copies.append(copy)
        ra_copies.append(copies)

    rb_copies = []

    def reduce_first(ch):
        ic = CHUNKS[ch][1]
        for copy in ra_copies[ch]:
            copy.wait_recv()
        if AX[ch] == 0:
            total = u[ch, :, pl.ds(w, 1)].reshape(4, 8, 512)
        else:
            total = u[ch, pl.ds(yl, 1)].reshape(4, 8, 512)
        sb[ch] = total + ra[ch, 0] + ra[ch, 1] + ra[ch, 2]
        copies = []
        for d in (2, 1, 3):
            to, n = (along_y(d), (yl + d) % 4) if AX[ch] == 0 else (along_z(d), (w + d) % 4)
            copy = remote(sb.at[ch, n], rb.at[ch, d - 1], rb_send.at[ch, d - 1], rb_recv.at[ch, d - 1], to)
            copy.start()
            copies.append(copy)
        rb_copies.append(copies)

    slot = (z // 4) * 4 + (z % 2) * 2 + (z // 2) % 2
    slot_rows = rows(8 * slot, 8)
    ag_copies = []

    def gather(ch):
        for copy in rb_copies[ch]:
            copy.wait_recv()
        own = yl if AX[ch] == 0 else w
        total = sb[ch, pl.ds(own, 1)].reshape(8, 512)
        ag[ch, slot_rows] = total + rb[ch, 0] + rb[ch, 1] + rb[ch, 2]
        copies = []
        for dz in (4, 3, 5, 2, 6, 1, 7):
            to = device(x, yh, k, yl, (z + dz) % 8)
            copy = remote(
                ag.at[ch, slot_rows], ag.at[ch, slot_rows], ag_send.at[ch, dz], ag_recv.at[ch, dz], to
            )
            copy.start()
            copies.append(copy)
        ag_copies.append(copies)

    reduce_first(0)
    reduce_first(1)
    pass_x(2)
    send_x(3)
    gather(0)
    reduce_first(2)
    gather(1)
    reduce_first(3)
    gather(2)
    gather(3)
    pass_x(3)

    own_x.wait()
    copy_xs.wait_recv()
    for sends, receives, copy, relay in x_hops:

        @pl.when(receives)
        def _(relay=relay):
            relay.wait_recv()

    finals = []
    fa_copies = []
    for tc in range(2):
        for ch in (2 * tc, 2 * tc + 1):
            for copy in ag_copies[ch]:
                copy.wait_recv()
        a = [split(ag[2 * tc + ic]) for ic in range(2)]
        copies = []
        for dx in (2, 1, 3, 0):
            if tc == 0:
                xs[0, dx], xs[1, dx] = split(xb[pl.ds((x + dx) % 4, 1)].reshape(2, 128, 512))
            op[tc, dx] = dot_nt(a[0], (xs[0, dx, 0], xs[1, dx, 0])) + dot_nt(
                a[1], (xs[0, dx, 1], xs[1, dx, 1])
            )
            if dx:
                copy = remote(
                    op.at[tc, dx], fa.at[tc, dx - 1],
                    fa_send.at[tc, dx - 1], fa_recv.at[tc, dx - 1], along_x(dx, 0),
                )
                copy.start()
                copies.append(copy)
        fa_copies.append(copies)

    core_out = (z // 2) % 2
    for tc in range(2):
        for copy in fa_copies[tc]:
            copy.wait_recv()
        fs[tc] = op[tc, 0] + fa[tc, 0] + fa[tc, 1] + fa[tc, 2]
        place = pl.ds(16 * tc, 16)
        for g in range(2):
            for q in range(2):
                n = 2 * g + q
                z_out = 4 * g + 2 * k + q
                here = jnp.logical_and(
                    jnp.logical_and(yh == z // 4, k == core_out), z == z_out
                )
                tile = pl.ds(16 * n, 16)
                copy = remote(
                    fs.at[tc, tile], fr.at[yh, z % 2, place],
                    f_send.at[tc, n], f_recv.at[tc, yh, z % 2],
                    device(x, z // 4, core_out, yl, z_out),
                )
                finals.append((here, copy))

                @pl.when(jnp.logical_not(here))
                def _(copy=copy):
                    copy.start()

                @pl.when(here)
                def _(tc=tc, tile=tile, place=place):
                    fr[yh, z % 2, place] = fs[tc, tile]

    for tc in range(2):
        place = pl.ds(16 * tc, 16)
        for half in range(2):
            for s in range(2):
                here = jnp.logical_and(
                    jnp.logical_and(yh == s, 4 * yh + 2 * k + half == z), k == core_out
                )
                arrival = remote(
                    fs.at[0, pl.ds(0, 16)], fr.at[s, half, place],
                    f_send.at[0, 0], f_recv.at[tc, s, half], sibling,
                )

                @pl.when(jnp.logical_not(here))
                def _(arrival=arrival):
                    arrival.wait_recv()

            o_ref[place, pl.ds(128 * half, 128)] = fr[0, half, place] + fr[1, half, place]

    copy_ty.wait_send()
    for copies in t_copies + ra_copies + rb_copies + ag_copies + fa_copies:
        for copy in copies:
            copy.wait_send()
    for sends, receives, copy, relay in x_hops:

        @pl.when(sends)
        def _(copy=copy):
            copy.wait_send()

        @pl.when(receives)
        def _(relay=relay):
            relay.wait_send()

    for copy in (copy_mp, copy_ms, copy_mr, copy_xs):
        copy.wait_send()
    for here, copy in finals:

        @pl.when(jnp.logical_not(here))
        def _(copy=copy):
            copy.wait_send()


def on_device(train_features, inverse, test_features):
    vmem = pltpu.VMEM
    dma = pltpu.SemaphoreType.DMA
    return pl.pallas_call(
        kernel,
        out_shape=jax.ShapeDtypeStruct((32, 256), F32),
        in_specs=[pl.BlockSpec(memory_space=pltpu.HBM)] * 3,
        out_specs=pl.BlockSpec(memory_space=pltpu.VMEM),
        scratch_shapes=[
            vmem((2, 2, 512, 256), F32),
            vmem((2, 2, 2, 512, 256), BF16),
            vmem((4, 2, 128, 512), F32),
            vmem((2, 4, 2, 128, 512), BF16),
            vmem((8, 8, 256), F32),
            vmem((3, 32, 8, 256), F32),
            vmem((4, 4, 4, 8, 512), F32),
            vmem((4, 3, 4, 8, 512), F32),
            vmem((4, 4, 8, 512), F32),
            vmem((4, 3, 8, 512), F32),
            vmem((4, 64, 512), F32),
            vmem((2, 4, 64, 128), F32),
            vmem((2, 3, 64, 128), F32),
            vmem((2, 64, 128), F32),
            vmem((2, 2, 32, 128), F32),
            dma((4,)),
            dma((3,)), dma((3,)),
            dma((13,)), dma((13,)),
            dma, dma,
            dma((24,)), dma((24,)),
            dma((4, 3)), dma((4, 3)),
            dma((4, 3)), dma((4, 3)),
            dma((4, 8)), dma((4, 8)),
            dma((2, 3)), dma((2, 3)),
            dma((2, 4)), dma((2, 2, 2)),
        ],
        compiler_params=pltpu.CompilerParams(
            collective_id=0, has_side_effects=True, vmem_limit_bytes=64 * 2**20 - 2**16
        ),
        cost_estimate=pl.CostEstimate(flops=1207959552, bytes_accessed=2 * 2**20, transcendentals=0),
        name="scores",
    )(train_features, inverse, test_features.reshape(8, 8, 256))


def solution(mesh):
    placed = (P("col", "row"), P("row", "col"), P("row", "col"))
    return jax.shard_map(
        on_device, mesh=mesh, in_specs=placed, out_specs=P("col", "row"), check_vma=False
    )
```

```python
import jax
import jax.numpy as jnp
from jax import lax
from jax.experimental import pallas as pl
from jax.experimental.pallas import tpu as pltpu
from jax.sharding import PartitionSpec as P

MESH = pl.DeviceIdType.MESH
F32 = jnp.float32
BF16 = jnp.bfloat16
AX = (0, 0, 1, 0)
CHUNKS = ((0, 0), (0, 1), (1, 0), (1, 1))


def split(value):
    high = value.astype(BF16)
    return high, (value - high.astype(F32)).astype(BF16)


def dot_nt(left, right):
    def product(a, b):
        return lax.dot_general(a, b, (((1,), (1,)), ((), ())), preferred_element_type=F32)

    return product(left[0], right[1]) + product(left[1], right[0]) + product(left[0], right[0])


def device(x, yh, core, yl, z):
    return ((x * 2 + yh) * 2 + core, yl * 8 + z)


def kernel(
    x_ref, m_ref, t_ref, o_ref,
    mb, ms, xb, xs, ty, tb, u, ra, sb, rb, ag, op, fa, fs, fr,
    local_sem, m_send, m_recv, x_send, x_recv, ty_send, ty_recv, t_send, t_recv,
    ra_send, ra_recv, rb_send, rb_recv, ag_send, ag_recv, fa_send, fa_recv, f_send, f_recv,
):
    r = lax.axis_index("row")
    c = lax.axis_index("col")
    k = r % 2
    yh = (r // 2) % 2
    x = r // 4
    rp = r // 2
    yl = c // 8
    z = c % 8
    p = z % 2
    w = z // 2
    step = (1 - 2 * p) * (1 - 2 * k)

    def remote(src, dst, send, recv, to):
        return pltpu.make_async_remote_copy(
            src_ref=src, dst_ref=dst, send_sem=send, recv_sem=recv, device_id=to, device_id_type=MESH
        )

    def rows(start, size):
        return pl.ds(pl.multiple_of(start, size), size)

    sibling = device(x, yh, 1 - k, yl, z)
    across = device(x, 1 - yh, k, yl, z)

    def along_x(dx, q):
        zz = (z, (z + step) % 8, (z - step) % 8)[q]
        return device((x + dx) % 4, yh, k, yl, zz)

    def along_y(d):
        return device(x, yh, k, (yl + d) % 4, z)

    def along_z(d):
        return device(x, yh, k, yl, 2 * ((w + d) % 4) + p)

    barrier = pltpu.get_barrier_semaphore()
    greeted = [across, sibling]
    greeted += [along_x(dx, q) for dx in range(4) for q in range(3) if dx or q]
    greeted += [along_y(d) for d in (1, 2, 3)] + [along_z(d) for d in (1, 2, 3)]
    for to in greeted:
        pl.semaphore_signal(barrier, inc=1, device_id=to, device_id_type=MESH)

    own_m = pltpu.make_async_copy(m_ref, mb.at[0, 0], local_sem.at[0])
    own_x = pltpu.make_async_copy(x_ref, xb.at[yl, 0], local_sem.at[1])
    own_t = pltpu.make_async_copy(t_ref.at[rows(4 * p, 4)], tb.at[0, rows(4 * rp, 4)], local_sem.at[2])
    own_m.start()
    own_x.start()
    own_t.start()

    pl.semaphore_wait(barrier, len(greeted))

    copy_ty = remote(t_ref, ty, ty_send, ty_recv, across)
    copy_ty.start()
    x_hops = []

    def send_x(hop):
        for way, side in enumerate((1, -1)):
            block = yl - side * (hop - 1)
            there = yl + side
            n = 3 * way + hop - 1
            sends = jnp.logical_and(
                jnp.logical_and(block >= 0, block <= 3), jnp.logical_and(there >= 0, there <= 3)
            )
            comes = yl - side * hop
            receives = jnp.logical_and(comes >= 0, comes <= 3)
            source = x_ref if hop == 1 else xb.at[jnp.clip(block, 0, 3), 0]
            copy = remote(
                source, xb.at[jnp.clip(block, 0, 3), 0], x_send.at[n], x_recv.at[n],
                device(x, yh, k, (yl + side) % 4, z),
            )
            slot = jnp.clip(comes, 0, 3)
            relay = remote(xb.at[slot, 0], xb.at[slot, 1], x_send.at[7 + n], x_recv.at[7 + n], sibling)
            x_hops.append((sends, receives, copy, relay))

            @pl.when(sends)
            def _(copy=copy):
                copy.start()

    def pass_x(hop):
        for sends, receives, copy, relay in x_hops[2 * hop - 2:2 * hop]:

            @pl.when(receives)
            def _(copy=copy, relay=relay):
                copy.wait_recv()
                relay.start()

    send_x(1)
    copy_xs = remote(x_ref, xb.at[yl, 1], x_send.at[6], x_recv.at[6], sibling)
    copy_xs.start()

    t_copies = [[], [], []]

    def send_t(block_ref, b):
        to_rows = rows(4 * (2 * x + (yh if b == 0 else 1 - yh)), 4)
        for dx in (2, 1, 3, 0):
            for q in (1, 0, 2):
                if dx == 0 and q == 0:
                    continue
                half = p if q == 0 else 1 - p
                n = (b * 4 + dx) * 3 + q
                copy = remote(
                    block_ref.at[rows(4 * half, 4)], tb.at[q, to_rows],
                    t_send.at[n], t_recv.at[n], along_x(dx, q),
                )
                copy.start()
                t_copies[q].append(copy)

    copy_mp = remote(m_ref, mb.at[1, 0], m_send.at[0], m_recv.at[0], along_x(0, 1))
    copy_mp.start()
    send_t(t_ref, 0)
    copy_ms = remote(m_ref, mb.at[0, 1], m_send.at[1], m_recv.at[1], sibling)
    copy_ms.start()
    copy_ty.wait_recv()
    send_t(ty, 1)
    own_ty = pltpu.make_async_copy(
        ty.at[rows(4 * p, 4)], tb.at[0, rows(4 * (2 * x + 1 - yh), 4)], local_sem.at[3]
    )
    own_ty.start()

    pass_x(1)
    send_x(2)
    made = set()

    def inverse_halves(j, ic):
        if (j, ic) not in made:
            made.add((j, ic))
            ms[0, j, ic], ms[1, j, ic] = split(mb[j, ic])
        return ms[0, j, ic], ms[1, j, ic]

    own_m.wait()
    inverse_halves(0, 0)
    copy_ms.wait_recv()
    inverse_halves(0, 1)

    own_t.wait()
    own_ty.wait()
    for copy in t_copies[0] + t_copies[1]:
        copy.wait_recv()
    copy_mp.wait_recv()
    copy_mr = remote(mb.at[1, 0], mb.at[1, 1], m_send.at[2], m_recv.at[2], sibling)
    copy_mr.start()

    ra_copies = []
    for ch, (tc, ic) in enumerate(CHUNKS):
        if ch == 1:
            for copy in t_copies[2]:
                copy.wait_recv()
            copy_mr.wait_recv()

        def test_rows(q):
            return split(tb[q].reshape(8, 2, 16, 256)[:, tc].reshape(128, 256))

        u[ch] = (
            dot_nt(test_rows(0), inverse_halves(0, ic)) + dot_nt(test_rows(1 + ic), inverse_halves(1, ic))
        ).reshape(4, 4, 8, 512)
        copies = []
        for d in (2, 1, 3):
            if AX[ch] == 0:
                to, part = along_z(d), u.at[ch, :, (w + d) % 4]
            else:
                to, part = along_y(d), u.at[ch, (yl + d) % 4]
            copy = remote(part, ra.at[ch, d - 1], ra_send.at[ch, d - 1], ra_recv.at[ch, d - 1], to)
            copy.start()
            copies.append(copy)
        ra_copies.append(copies)

    rb_copies = []

    def reduce_first(ch):
        ic = CHUNKS[ch][1]
        for copy in ra_copies[ch]:
            copy.wait_recv()
        if AX[ch] == 0:
            total = u[ch, :, pl.ds(w, 1)].reshape(4, 8, 512)
        else:
            total = u[ch, pl.ds(yl, 1)].reshape(4, 8, 512)
        sb[ch] = total + ra[ch, 0] + ra[ch, 1] + ra[ch, 2]
        copies = []
        for d in (2, 1, 3):
            to, n = (along_y(d), (yl + d) % 4) if AX[ch] == 0 else (along_z(d), (w + d) % 4)
            copy = remote(sb.at[ch, n], rb.at[ch, d - 1], rb_send.at[ch, d - 1], rb_recv.at[ch, d - 1], to)
            copy.start()
            copies.append(copy)
        rb_copies.append(copies)

    slot = (z // 4) * 4 + (z % 2) * 2 + (z // 2) % 2
    slot_rows = rows(8 * slot, 8)
    ag_copies = []

    def gather(ch):
        for copy in rb_copies[ch]:
            copy.wait_recv()
        own = yl if AX[ch] == 0 else w
        total = sb[ch, pl.ds(own, 1)].reshape(8, 512)
        ag[ch, slot_rows] = total + rb[ch, 0] + rb[ch, 1] + rb[ch, 2]
        copies = []
        for dz in (4, 3, 5, 2, 6, 1, 7):
            to = device(x, yh, k, yl, (z + dz) % 8)
            copy = remote(
                ag.at[ch, slot_rows], ag.at[ch, slot_rows], ag_send.at[ch, dz], ag_recv.at[ch, dz], to
            )
            copy.start()
            copies.append(copy)
        ag_copies.append(copies)

    reduce_first(0)
    reduce_first(1)
    gather(0)
    pass_x(2)
    send_x(3)
    reduce_first(2)
    gather(1)
    reduce_first(3)
    gather(2)
    gather(3)
    pass_x(3)

    own_x.wait()
    copy_xs.wait_recv()
    for sends, receives, copy, relay in x_hops:

        @pl.when(receives)
        def _(relay=relay):
            relay.wait_recv()

    finals = []
    fa_copies = []
    for tc in range(2):
        for ch in (2 * tc, 2 * tc + 1):
            for copy in ag_copies[ch]:
                copy.wait_recv()
        a = [split(ag[2 * tc + ic]) for ic in range(2)]
        copies = []
        for dx in (2, 1, 3, 0):
            if tc == 0:
                xs[0, dx], xs[1, dx] = split(xb[pl.ds((x + dx) % 4, 1)].reshape(2, 128, 512))
            op[tc, dx] = dot_nt(a[0], (xs[0, dx, 0], xs[1, dx, 0])) + dot_nt(
                a[1], (xs[0, dx, 1], xs[1, dx, 1])
            )
            if dx:
                copy = remote(
                    op.at[tc, dx], fa.at[tc, dx - 1],
                    fa_send.at[tc, dx - 1], fa_recv.at[tc, dx - 1], along_x(dx, 0),
                )
                copy.start()
                copies.append(copy)
        fa_copies.append(copies)

    core_out = (z // 2) % 2
    for tc in range(2):
        for copy in fa_copies[tc]:
            copy.wait_recv()
        fs[tc] = op[tc, 0] + fa[tc, 0] + fa[tc, 1] + fa[tc, 2]
        place = pl.ds(16 * tc, 16)
        for g in range(2):
            for q in range(2):
                n = 2 * g + q
                z_out = 4 * g + 2 * k + q
                here = jnp.logical_and(
                    jnp.logical_and(yh == z // 4, k == core_out), z == z_out
                )
                tile = pl.ds(16 * n, 16)
                copy = remote(
                    fs.at[tc, tile], fr.at[yh, z % 2, place],
                    f_send.at[tc, n], f_recv.at[tc, yh, z % 2],
                    device(x, z // 4, core_out, yl, z_out),
                )
                finals.append((here, copy))

                @pl.when(jnp.logical_not(here))
                def _(copy=copy):
                    copy.start()

                @pl.when(here)
                def _(tc=tc, tile=tile, place=place):
                    fr[yh, z % 2, place] = fs[tc, tile]

    for tc in range(2):
        place = pl.ds(16 * tc, 16)
        for half in range(2):
            for s in range(2):
                here = jnp.logical_and(
                    jnp.logical_and(yh == s, 4 * yh + 2 * k + half == z), k == core_out
                )
                arrival = remote(
                    fs.at[0, pl.ds(0, 16)], fr.at[s, half, place],
                    f_send.at[0, 0], f_recv.at[tc, s, half], sibling,
                )

                @pl.when(jnp.logical_not(here))
                def _(arrival=arrival):
                    arrival.wait_recv()

            o_ref[place, pl.ds(128 * half, 128)] = fr[0, half, place] + fr[1, half, place]

    copy_ty.wait_send()
    for copies in t_copies + ra_copies + rb_copies + ag_copies + fa_copies:
        for copy in copies:
            copy.wait_send()
    for sends, receives, copy, relay in x_hops:

        @pl.when(sends)
        def _(copy=copy):
            copy.wait_send()

        @pl.when(receives)
        def _(relay=relay):
            relay.wait_send()

    for copy in (copy_mp, copy_ms, copy_mr, copy_xs):
        copy.wait_send()
    for here, copy in finals:

        @pl.when(jnp.logical_not(here))
        def _(copy=copy):
            copy.wait_send()


def on_device(train_features, inverse, test_features):
    vmem = pltpu.VMEM
    dma = pltpu.SemaphoreType.DMA
    return pl.pallas_call(
        kernel,
        out_shape=jax.ShapeDtypeStruct((32, 256), F32),
        in_specs=[pl.BlockSpec(memory_space=pltpu.HBM)] * 3,
        out_specs=pl.BlockSpec(memory_space=pltpu.VMEM),
        scratch_shapes=[
            vmem((2, 2, 512, 256), F32),
            vmem((2, 2, 2, 512, 256), BF16),
            vmem((4, 2, 128, 512), F32),
            vmem((2, 4, 2, 128, 512), BF16),
            vmem((8, 8, 256), F32),
            vmem((3, 32, 8, 256), F32),
            vmem((4, 4, 4, 8, 512), F32),
            vmem((4, 3, 4, 8, 512), F32),
            vmem((4, 4, 8, 512), F32),
            vmem((4, 3, 8, 512), F32),
            vmem((4, 64, 512), F32),
            vmem((2, 4, 64, 128), F32),
            vmem((2, 3, 64, 128), F32),
            vmem((2, 64, 128), F32),
            vmem((2, 2, 32, 128), F32),
            dma((4,)),
            dma((3,)), dma((3,)),
            dma((13,)), dma((13,)),
            dma, dma,
            dma((24,)), dma((24,)),
            dma((4, 3)), dma((4, 3)),
            dma((4, 3)), dma((4, 3)),
            dma((4, 8)), dma((4, 8)),
            dma((2, 3)), dma((2, 3)),
            dma((2, 4)), dma((2, 2, 2)),
        ],
        compiler_params=pltpu.CompilerParams(
            collective_id=0, has_side_effects=True, vmem_limit_bytes=64 * 2**20 - 2**16
        ),
        cost_estimate=pl.CostEstimate(flops=1207959552, bytes_accessed=2 * 2**20, transcendentals=0),
        name="scores",
    )(train_features, inverse, test_features.reshape(8, 8, 256))


def solution(mesh):
    placed = (P("col", "row"), P("row", "col"), P("row", "col"))
    return jax.shard_map(
        on_device, mesh=mesh, in_specs=placed, out_specs=P("col", "row"), check_vma=False
    )
```

```python
import jax
import jax.numpy as jnp
from jax import lax
from jax.experimental import pallas as pl
from jax.experimental.pallas import tpu as pltpu
from jax.sharding import PartitionSpec as P

MESH = pl.DeviceIdType.MESH
F32 = jnp.float32
BF16 = jnp.bfloat16
AX = (0, 1, 0, 0)
CHUNKS = ((0, 0), (0, 1), (1, 0), (1, 1))


def split(value):
    high = value.astype(BF16)
    return high, (value - high.astype(F32)).astype(BF16)


def dot_nt(left, right):
    def product(a, b):
        return lax.dot_general(a, b, (((1,), (1,)), ((), ())), preferred_element_type=F32)

    return product(left[0], right[1]) + product(left[1], right[0]) + product(left[0], right[0])


def device(x, yh, core, yl, z):
    return ((x * 2 + yh) * 2 + core, yl * 8 + z)


def kernel(
    x_ref, m_ref, t_ref, o_ref,
    mb, ms, xb, xs, ty, tb, u, ra, sb, rb, ag, op, fa, fs, fr,
    local_sem, m_send, m_recv, x_send, x_recv, ty_send, ty_recv, t_send, t_recv,
    ra_send, ra_recv, rb_send, rb_recv, ag_send, ag_recv, fa_send, fa_recv, f_send, f_recv,
):
    r = lax.axis_index("row")
    c = lax.axis_index("col")
    k = r % 2
    yh = (r // 2) % 2
    x = r // 4
    rp = r // 2
    yl = c // 8
    z = c % 8
    p = z % 2
    w = z // 2
    step = (1 - 2 * p) * (1 - 2 * k)

    def remote(src, dst, send, recv, to):
        return pltpu.make_async_remote_copy(
            src_ref=src, dst_ref=dst, send_sem=send, recv_sem=recv, device_id=to, device_id_type=MESH
        )

    def rows(start, size):
        return pl.ds(pl.multiple_of(start, size), size)

    sibling = device(x, yh, 1 - k, yl, z)
    across = device(x, 1 - yh, k, yl, z)

    def along_x(dx, q):
        zz = (z, (z + step) % 8, (z - step) % 8)[q]
        return device((x + dx) % 4, yh, k, yl, zz)

    def along_y(d):
        return device(x, yh, k, (yl + d) % 4, z)

    def along_z(d):
        return device(x, yh, k, yl, 2 * ((w + d) % 4) + p)

    barrier = pltpu.get_barrier_semaphore()
    greeted = [across, sibling]
    greeted += [along_x(dx, q) for dx in range(4) for q in range(3) if dx or q]
    greeted += [along_y(d) for d in (1, 2, 3)] + [along_z(d) for d in (1, 2, 3)]
    for to in greeted:
        pl.semaphore_signal(barrier, inc=1, device_id=to, device_id_type=MESH)

    own_m = pltpu.make_async_copy(m_ref, mb.at[0, 0], local_sem.at[0])
    own_x = pltpu.make_async_copy(x_ref, xb.at[yl, 0], local_sem.at[1])
    own_t = pltpu.make_async_copy(t_ref.at[rows(4 * p, 4)], tb.at[0, rows(4 * rp, 4)], local_sem.at[2])
    own_m.start()
    own_x.start()
    own_t.start()

    pl.semaphore_wait(barrier, len(greeted))

    copy_ty = remote(t_ref, ty, ty_send, ty_recv, across)
    copy_ty.start()
    x_hops = []

    def send_x(hop):
        for way, side in enumerate((1, -1)):
            block = yl - side * (hop - 1)
            there = yl + side
            n = 3 * way + hop - 1
            sends = jnp.logical_and(
                jnp.logical_and(block >= 0, block <= 3), jnp.logical_and(there >= 0, there <= 3)
            )
            comes = yl - side * hop
            receives = jnp.logical_and(comes >= 0, comes <= 3)
            source = x_ref if hop == 1 else xb.at[jnp.clip(block, 0, 3), 0]
            copy = remote(
                source, xb.at[jnp.clip(block, 0, 3), 0], x_send.at[n], x_recv.at[n],
                device(x, yh, k, (yl + side) % 4, z),
            )
            slot = jnp.clip(comes, 0, 3)
            relay = remote(xb.at[slot, 0], xb.at[slot, 1], x_send.at[7 + n], x_recv.at[7 + n], sibling)
            x_hops.append((sends, receives, copy, relay))

            @pl.when(sends)
            def _(copy=copy):
                copy.start()

    def pass_x(hop):
        for sends, receives, copy, relay in x_hops[2 * hop - 2:2 * hop]:

            @pl.when(receives)
            def _(copy=copy, relay=relay):
                copy.wait_recv()
                relay.start()

    send_x(1)
    copy_xs = remote(x_ref, xb.at[yl, 1], x_send.at[6], x_recv.at[6], sibling)
    copy_xs.start()

    t_copies = [[], [], []]

    def send_t(block_ref, b):
        to_rows = rows(4 * (2 * x + (yh if b == 0 else 1 - yh)), 4)
        for dx in (2, 1, 3, 0):
            for q in (1, 0, 2):
                if dx == 0 and q == 0:
                    continue
                half = p if q == 0 else 1 - p
                n = (b * 4 + dx) * 3 + q
                copy = remote(
                    block_ref.at[rows(4 * half, 4)], tb.at[q, to_rows],
                    t_send.at[n], t_recv.at[n], along_x(dx, q),
                )
                copy.start()
                t_copies[q].append(copy)

    copy_mp = remote(m_ref, mb.at[1, 0], m_send.at[0], m_recv.at[0], along_x(0, 1))
    copy_mp.start()
    send_t(t_ref, 0)
    copy_ms = remote(m_ref, mb.at[0, 1], m_send.at[1], m_recv.at[1], sibling)
    copy_ms.start()
    copy_ty.wait_recv()
    send_t(ty, 1)
    own_ty = pltpu.make_async_copy(
        ty.at[rows(4 * p, 4)], tb.at[0, rows(4 * (2 * x + 1 - yh), 4)], local_sem.at[3]
    )
    own_ty.start()

    pass_x(1)
    send_x(2)
    made = set()

    def inverse_halves(j, ic):
        if (j, ic) not in made:
            made.add((j, ic))
            ms[0, j, ic], ms[1, j, ic] = split(mb[j, ic])
        return ms[0, j, ic], ms[1, j, ic]

    own_m.wait()
    inverse_halves(0, 0)
    copy_ms.wait_recv()
    inverse_halves(0, 1)

    own_t.wait()
    own_ty.wait()
    for copy in t_copies[0] + t_copies[1]:
        copy.wait_recv()
    copy_mp.wait_recv()
    copy_mr = remote(mb.at[1, 0], mb.at[1, 1], m_send.at[2], m_recv.at[2], sibling)
    copy_mr.start()

    ra_copies = []
    for ch, (tc, ic) in enumerate(CHUNKS):
        if ch == 1:
            for copy in t_copies[2]:
                copy.wait_recv()
            copy_mr.wait_recv()

        def test_rows(q):
            return split(tb[q].reshape(8, 2, 16, 256)[:, tc].reshape(128, 256))

        u[ch] = (
            dot_nt(test_rows(0), inverse_halves(0, ic)) + dot_nt(test_rows(1 + ic), inverse_halves(1, ic))
        ).reshape(4, 4, 8, 512)
        copies = []
        for d in (2, 1, 3):
            if AX[ch] == 0:
                to, part = along_z(d), u.at[ch, :, (w + d) % 4]
            else:
                to, part = along_y(d), u.at[ch, (yl + d) % 4]
            copy = remote(part, ra.at[ch, d - 1], ra_send.at[ch, d - 1], ra_recv.at[ch, d - 1], to)
            copy.start()
            copies.append(copy)
        ra_copies.append(copies)

    rb_copies = []

    def reduce_first(ch):
        ic = CHUNKS[ch][1]
        for copy in ra_copies[ch]:
            copy.wait_recv()
        if AX[ch] == 0:
            total = u[ch, :, pl.ds(w, 1)].reshape(4, 8, 512)
        else:
            total = u[ch, pl.ds(yl, 1)].reshape(4, 8, 512)
        sb[ch] = total + ra[ch, 0] + ra[ch, 1] + ra[ch, 2]
        copies = []
        for d in (2, 1, 3):
            to, n = (along_y(d), (yl + d) % 4) if AX[ch] == 0 else (along_z(d), (w + d) % 4)
            copy = remote(sb.at[ch, n], rb.at[ch, d - 1], rb_send.at[ch, d - 1], rb_recv.at[ch, d - 1], to)
            copy.start()
            copies.append(copy)
        rb_copies.append(copies)

    slot = (z // 4) * 4 + (z % 2) * 2 + (z // 2) % 2
    slot_rows = rows(8 * slot, 8)
    ag_copies = []

    def gather(ch):
        for copy in rb_copies[ch]:
            copy.wait_recv()
        own = yl if AX[ch] == 0 else w
        total = sb[ch, pl.ds(own, 1)].reshape(8, 512)
        ag[ch, slot_rows] = total + rb[ch, 0] + rb[ch, 1] + rb[ch, 2]
        copies = []
        for dz in (4, 3, 5, 2, 6, 1, 7):
            to = device(x, yh, k, yl, (z + dz) % 8)
            copy = remote(
                ag.at[ch, slot_rows], ag.at[ch, slot_rows], ag_send.at[ch, dz], ag_recv.at[ch, dz], to
            )
            copy.start()
            copies.append(copy)
        ag_copies.append(copies)

    reduce_first(0)
    reduce_first(1)
    pass_x(2)
    send_x(3)
    gather(0)
    reduce_first(2)
    gather(1)
    reduce_first(3)
    gather(2)
    gather(3)
    pass_x(3)

    own_x.wait()
    copy_xs.wait_recv()
    for sends, receives, copy, relay in x_hops:

        @pl.when(receives)
        def _(relay=relay):
            relay.wait_recv()

    finals = []
    fa_copies = []
    for tc in range(2):
        for ch in (2 * tc, 2 * tc + 1):
            for copy in ag_copies[ch]:
                copy.wait_recv()
        a = [split(ag[2 * tc + ic]) for ic in range(2)]
        copies = []
        for dx in (2, 1, 3, 0):
            if tc == 0:
                xs[0, dx], xs[1, dx] = split(xb[pl.ds((x + dx) % 4, 1)].reshape(2, 128, 512))
            op[tc, dx] = dot_nt(a[0], (xs[0, dx, 0], xs[1, dx, 0])) + dot_nt(
                a[1], (xs[0, dx, 1], xs[1, dx, 1])
            )
            if dx:
                copy = remote(
                    op.at[tc, dx], fa.at[tc, dx - 1],
                    fa_send.at[tc, dx - 1], fa_recv.at[tc, dx - 1], along_x(dx, 0),
                )
                copy.start()
                copies.append(copy)
        fa_copies.append(copies)

    core_out = (z // 2) % 2
    for tc in range(2):
        for copy in fa_copies[tc]:
            copy.wait_recv()
        fs[tc] = op[tc, 0] + fa[tc, 0] + fa[tc, 1] + fa[tc, 2]
        place = pl.ds(16 * tc, 16)
        for g in range(2):
            for q in range(2):
                n = 2 * g + q
                z_out = 4 * g + 2 * k + q
                here = jnp.logical_and(
                    jnp.logical_and(yh == z // 4, k == core_out), z == z_out
                )
                tile = pl.ds(16 * n, 16)
                copy = remote(
                    fs.at[tc, tile], fr.at[yh, z % 2, place],
                    f_send.at[tc, n], f_recv.at[tc, yh, z % 2],
                    device(x, z // 4, core_out, yl, z_out),
                )
                finals.append((here, copy))

                @pl.when(jnp.logical_not(here))
                def _(copy=copy):
                    copy.start()

                @pl.when(here)
                def _(tc=tc, tile=tile, place=place):
                    fr[yh, z % 2, place] = fs[tc, tile]

    for tc in range(2):
        place = pl.ds(16 * tc, 16)
        for half in range(2):
            for s in range(2):
                here = jnp.logical_and(
                    jnp.logical_and(yh == s, 4 * yh + 2 * k + half == z), k == core_out
                )
                arrival = remote(
                    fs.at[0, pl.ds(0, 16)], fr.at[s, half, place],
                    f_send.at[0, 0], f_recv.at[tc, s, half], sibling,
                )

                @pl.when(jnp.logical_not(here))
                def _(arrival=arrival):
                    arrival.wait_recv()

            o_ref[place, pl.ds(128 * half, 128)] = fr[0, half, place] + fr[1, half, place]

    copy_ty.wait_send()
    for copies in t_copies + ra_copies + rb_copies + ag_copies + fa_copies:
        for copy in copies:
            copy.wait_send()
    for sends, receives, copy, relay in x_hops:

        @pl.when(sends)
        def _(copy=copy):
            copy.wait_send()

        @pl.when(receives)
        def _(relay=relay):
            relay.wait_send()

    for copy in (copy_mp, copy_ms, copy_mr, copy_xs):
        copy.wait_send()
    for here, copy in finals:

        @pl.when(jnp.logical_not(here))
        def _(copy=copy):
            copy.wait_send()


def on_device(train_features, inverse, test_features):
    vmem = pltpu.VMEM
    dma = pltpu.SemaphoreType.DMA
    return pl.pallas_call(
        kernel,
        out_shape=jax.ShapeDtypeStruct((32, 256), F32),
        in_specs=[pl.BlockSpec(memory_space=pltpu.HBM)] * 3,
        out_specs=pl.BlockSpec(memory_space=pltpu.VMEM),
        scratch_shapes=[
            vmem((2, 2, 512, 256), F32),
            vmem((2, 2, 2, 512, 256), BF16),
            vmem((4, 2, 128, 512), F32),
            vmem((2, 4, 2, 128, 512), BF16),
            vmem((8, 8, 256), F32),
            vmem((3, 32, 8, 256), F32),
            vmem((4, 4, 4, 8, 512), F32),
            vmem((4, 3, 4, 8, 512), F32),
            vmem((4, 4, 8, 512), F32),
            vmem((4, 3, 8, 512), F32),
            vmem((4, 64, 512), F32),
            vmem((2, 4, 64, 128), F32),
            vmem((2, 3, 64, 128), F32),
            vmem((2, 64, 128), F32),
            vmem((2, 2, 32, 128), F32),
            dma((4,)),
            dma((3,)), dma((3,)),
            dma((13,)), dma((13,)),
            dma, dma,
            dma((24,)), dma((24,)),
            dma((4, 3)), dma((4, 3)),
            dma((4, 3)), dma((4, 3)),
            dma((4, 8)), dma((4, 8)),
            dma((2, 3)), dma((2, 3)),
            dma((2, 4)), dma((2, 2, 2)),
        ],
        compiler_params=pltpu.CompilerParams(
            collective_id=0, has_side_effects=True, vmem_limit_bytes=64 * 2**20 - 2**16
        ),
        cost_estimate=pl.CostEstimate(flops=1207959552, bytes_accessed=2 * 2**20, transcendentals=0),
        name="scores",
    )(train_features, inverse, test_features.reshape(8, 8, 256))


def solution(mesh):
    placed = (P("col", "row"), P("row", "col"), P("row", "col"))
    return jax.shard_map(
        on_device, mesh=mesh, in_specs=placed, out_specs=P("col", "row"), check_vma=False
    )
```
